512 devices in a mesh: wide: 64 (over z, y_hi, x), narrow: 8 (over y_lo, core).
Axes of the slice: x: 4, y: 8 (y_hi: 2, y_lo: 4; y = y_hi * 4 + y_lo), z: 8, core: 2. Of those that a mesh axis runs over, the one named last changes fastest.
Arguments:
- fine_field: float32 [256, 16, 32, 128], P('wide', 'narrow'), may hold values from -2.5 to 2.5
- fine_counts: int32 [256, 16, 128], P('wide', 'narrow'), may hold values from 1 to 8
- fine_offset: float32 [256, 16, 128], P('wide', 'narrow'), may hold values from 0.3 to 1.8
- kriging: float32 [256, 16, 128, 896], P('wide', 'narrow'), may hold values from -0.1875 to 0.1875
- whiten: float32 [256, 16, 128, 128], P('wide', 'narrow'), may hold values from -2 to 2
- neighbours: int32 [256, 16, 4], P('wide', 'narrow'), may hold values from 0 to 4095, as said below
- coarse_list: int32 [256, 16, 3], P('wide', 'narrow'), may hold values from 0 to 127, as said below
- coarse_field: float32 [128, 32, 128], P('wide'), may hold values from -2.5 to 2.5
- coarse_counts: int32 [128, 128], P('wide'), may hold values from 1 to 8
- coarse_offset: float32 [128, 128], P('wide'), may hold values from 0.3 to 1.8
- coarse_whiten: float32 [128, 128, 128], P('wide'), may hold values from -2 to 2
- coarse_home: int32 [128], replicated, may hold values from 0 to 127, each once
Outputs:
- fine_grad: float32 [256, 16, 32, 128], P('wide', 'narrow')
- coarse_grad: float32 [128, 32, 128], P('wide')
The draws below stay inside these ranges and needn't reach their ends.
Inputs may be any that keep to these rules, and one draw needn't show every extreme that they name: `neighbours`: entry [a, b, k] is the number of one of the eight blocks around block (a, b): rows a - 1, a or a + 1 modulo 256, columns b - 1, b or b + 1 modulo 16, not the block itself; the 4 entries of a block differ. `coarse_list`: the 3 entries of a fine block are different coarse block numbers.
All inputs are finite; a program needn't handle non-finite values.
Results may differ from the reference program's by a relative error of at most 0.0001.
Values sent between devices are 32-bit elements; how exact they have to be, the bound alone decides.
A program may use at most 64 MiB of HBM per device.

```python
import math
import jax
import jax.numpy as jnp
from jax import lax

BLOCK_SITES = 128
CHAIN_SPOTS = 32
NEIGHBOUR_BLOCKS = 4
COARSE_PER_BLOCK = 3
GX = 256
SHORT_BLOCKS = 16
NC = 128
COND = 896


STEP_ROWS = (-1, -1, -1, 0, 0, 1, 1, 1)


STEP_COLS = (-1, 0, 1, -1, 1, -1, 0, 1)


def whitening(key, leading):
    first_key = jax.random.fold_in(key, 11)
    second_key = jax.random.fold_in(key, 23)
    diagonal = jnp.exp(jax.random.uniform(first_key, leading + (BLOCK_SITES, 1), jnp.float32, math.log(0.7), math.log(1.4)))
    noise = jnp.clip(jax.random.normal(second_key, leading + (BLOCK_SITES, BLOCK_SITES), jnp.float32), -4.0, 4.0)
    identity = (jnp.arange(BLOCK_SITES)[:, None] == jnp.arange(BLOCK_SITES)[None, :]).astype(jnp.float32)
    return identity * diagonal + noise * (0.35 / math.sqrt(BLOCK_SITES))


def draw_whiten(key, part):
    return whitening(key, (GX, SHORT_BLOCKS))


def draw_coarse_whiten(key, part):
    return whitening(key, (NC,))


def draw_neighbours(key, part):
    ranking_values = jax.random.randint(jax.random.fold_in(key, 5), (GX, SHORT_BLOCKS, 8), 0, 1 << 20) * 8 + jnp.arange(8, dtype=jnp.int32)
    unused_slot, places = lax.top_k(ranking_values, NEIGHBOUR_BLOCKS)
    step_rows = jnp.array(STEP_ROWS, dtype=jnp.int32)[places]
    step_cols = jnp.array(STEP_COLS, dtype=jnp.int32)[places]
    rows = (jnp.arange(GX, dtype=jnp.int32)[:, None, None] + step_rows) % GX
    cols = (jnp.arange(SHORT_BLOCKS, dtype=jnp.int32)[None, :, None] + step_cols) % SHORT_BLOCKS
    return (rows * SHORT_BLOCKS + cols).astype(jnp.int32)


def draw_coarse_list(key, part):
    ranking_values = jax.random.randint(jax.random.fold_in(key, 7), (GX, SHORT_BLOCKS, NC), 0, 1 << 20) * NC + jnp.arange(NC, dtype=jnp.int32)
    unused_slot, picked_ids = lax.top_k(ranking_values, COARSE_PER_BLOCK)
    return picked_ids.astype(jnp.int32)


def with_ends(values, rng, low, largest):
    spot = [jax.random.randint(jax.random.fold_in(rng, axis), (), 0, length) for axis, length in enumerate(values.shape)]
    longest = values.shape.index(max(values.shape))
    beside = spot[:longest] + [(spot[longest] + 1) % values.shape[longest]] + spot[longest + 1:]
    return values.at[tuple(spot)].set(low).at[tuple(beside)].set(largest)


def steps_of(stream_key, extent, cuts, low, top_value):
    gain = 1.0
    for position, blocks in cuts:
        draws = jax.random.uniform(jax.random.fold_in(jax.random.fold_in(stream_key, 6), position), (blocks,), jnp.float32, low / len(cuts), top_value / len(cuts))
        gain = gain * jnp.repeat(jnp.exp(draws), extent[position] // blocks).reshape((-1,) + (1,) * (len(extent) - 1 - position))
    return gain


def normal_values(rng, extent, width, reach, shards=(), held_as=jnp.bfloat16):
    entries = jax.random.normal(rng, extent, jnp.float32) * width
    if len(shards) > 0:
        entries = steps_of(rng, extent, shards, -0.22, 0.18) * entries
    return jnp.clip(entries, min=-reach, max=reach).astype(held_as)


def setup_inputs(seed: int = 0) -> dict:
    keys = jax.random.split(jax.random.key(seed), 13)
    fine_field = normal_values(keys[0], (GX, SHORT_BLOCKS, CHAIN_SPOTS, BLOCK_SITES), 0.5, 2.5, ((0, 64), (1, 8)), jnp.float32)
    fine_counts = with_ends(jax.random.randint(keys[1], (GX, SHORT_BLOCKS, BLOCK_SITES), 1, 9), jax.random.fold_in(keys[1], 1), 1, 8).astype(jnp.int32)
    fine_offset = jnp.clip(0.3 + 1.5 * jax.random.uniform(keys[2], (GX, SHORT_BLOCKS, BLOCK_SITES), jnp.float32) ** steps_of(keys[2], (GX, SHORT_BLOCKS, BLOCK_SITES), ((0, 64), (1, 8)), -0.2, 0.2), 0.3, 1.8)
    kriging = normal_values(keys[3], (GX, SHORT_BLOCKS, BLOCK_SITES, COND), COND ** -0.5, 0.1875, ((0, 64), (1, 8)), jnp.float32)
    whiten = draw_whiten(jax.random.fold_in(keys[12], 71), 0)
    neighbours = draw_neighbours(jax.random.fold_in(keys[12], 71), 0)
    coarse_list = draw_coarse_list(jax.random.fold_in(keys[12], 71), 0)
    coarse_field = normal_values(keys[7], (NC, CHAIN_SPOTS, BLOCK_SITES), 0.5, 2.5, ((0, 64),), jnp.float32)
    coarse_counts = with_ends(jax.random.randint(keys[8], (NC, BLOCK_SITES), 1, 9), jax.random.fold_in(keys[8], 1), 1, 8).astype(jnp.int32)
    coarse_offset = jnp.clip(0.3 + 1.5 * jax.random.uniform(keys[9], (NC, BLOCK_SITES), jnp.float32) ** steps_of(keys[9], (NC, BLOCK_SITES), ((0, 64),), -0.2, 0.2), 0.3, 1.8)
    coarse_whiten = draw_coarse_whiten(jax.random.fold_in(keys[12], 71), 0)
    coarse_home = jax.random.permutation(keys[11], NC).astype(jnp.int32)
    return dict(fine_field=fine_field, fine_counts=fine_counts, fine_offset=fine_offset, kriging=kriging, whiten=whiten, neighbours=neighbours, coarse_list=coarse_list, coarse_field=coarse_field, coarse_counts=coarse_counts, coarse_offset=coarse_offset, coarse_whiten=coarse_whiten, coarse_home=coarse_home)


SHAPE_K = 1.25
EXACT = lax.Precision.HIGHEST

def weibull_grad(field, counts, offset):
    log_counts = jnp.log(counts.astype(jnp.float32))
    return SHAPE_K * (jnp.exp(SHAPE_K * (log_counts[..., None, :] - offset[..., None, :] - field)) - 1.0)

def reference(fine_field, fine_counts, fine_offset, kriging, whiten, neighbours, coarse_list, coarse_field, coarse_counts, coarse_offset, coarse_whiten, coarse_home):
    flat = fine_field.reshape(GX * SHORT_BLOCKS, CHAIN_SPOTS, BLOCK_SITES)
    by_number = coarse_field[coarse_home]
    joined_blocks = NEIGHBOUR_BLOCKS + COARSE_PER_BLOCK

    def one_row(carry, index):
        fine_acc, coarse_accumulated = carry
        near_ids = neighbours[index]
        distant_ids = coarse_list[index]
        condition = jnp.concatenate([flat[near_ids], by_number[distant_ids]], axis=1)
        weights = kriging[index].reshape(SHORT_BLOCKS, BLOCK_SITES, joined_blocks, BLOCK_SITES)
        predicted = jnp.einsum('gkcm,gskm->gcs', condition, weights, precision=EXACT)
        residual = fine_field[index] - predicted
        whitened = jnp.einsum('gcs,gts->gct', residual, whiten[index], precision=EXACT)
        back_white = jnp.einsum('gct,gts->gcs', whitened, whiten[index], precision=EXACT)
        handed_back = jnp.einsum('gcs,gskm->gkcm', back_white, weights, precision=EXACT)
        fine_acc = fine_acc.at[near_ids.reshape(-1)].add(handed_back[:, :NEIGHBOUR_BLOCKS].reshape(SHORT_BLOCKS * NEIGHBOUR_BLOCKS, CHAIN_SPOTS, BLOCK_SITES))
        own_ids = index * SHORT_BLOCKS + jnp.arange(SHORT_BLOCKS, dtype=jnp.int32)
        fine_acc = fine_acc.at[own_ids].add(-back_white)
        coarse_accumulated = coarse_accumulated.at[distant_ids.reshape(-1)].add(handed_back[:, NEIGHBOUR_BLOCKS:].reshape(SHORT_BLOCKS * COARSE_PER_BLOCK, CHAIN_SPOTS, BLOCK_SITES))
        return ((fine_acc, coarse_accumulated), None)
    start_fine = jnp.zeros((GX * SHORT_BLOCKS, CHAIN_SPOTS, BLOCK_SITES), fine_field.dtype)
    start_coarse = jnp.zeros((NC, CHAIN_SPOTS, BLOCK_SITES), fine_field.dtype)
    (fine_acc, coarse_accumulated), unused_slot = lax.scan(one_row, (start_fine, start_coarse), jnp.arange(GX, dtype=jnp.int32))
    fine_grad = weibull_grad(fine_field, fine_counts, fine_offset) + fine_acc.reshape(GX, SHORT_BLOCKS, CHAIN_SPOTS, BLOCK_SITES)
    readers = jnp.zeros((NC, CHAIN_SPOTS, BLOCK_SITES), fine_field.dtype).at[coarse_home].set(coarse_accumulated)
    whitened_far = jnp.einsum('ncs,nts->nct', coarse_field, coarse_whiten, precision=EXACT)
    prior_far = jnp.einsum('nct,nts->ncs', whitened_far, coarse_whiten, precision=EXACT)
    coarse_grad = weibull_grad(coarse_field, coarse_counts, coarse_offset) - prior_far + readers
    return (fine_grad, coarse_grad)
```

```python
import functools

import jax
import jax.numpy as jnp
from jax import lax
from jax.experimental import pallas as pl
from jax.experimental.pallas import tpu as pltpu
from jax.sharding import PartitionSpec as P

SHAPE_K = 1.25
EXACT = lax.Precision.HIGHEST
MESH = pl.DeviceIdType.MESH
NT = (((1,), (1,)), ((), ()))
NN = (((1,), (0,)), ((), ()))
TN = (((0,), (0,)), ((), ()))
PLACES = ((-1, -1), (-1, 0), (-1, 1), (0, -1), (0, 1), (1, -1), (1, 0), (1, 1))

SLICES = 8
GROUP = 8


def weibull(field, counts, offset):
    return SHAPE_K * (
        jnp.exp(SHAPE_K * (jnp.log(counts.astype(jnp.float32)) - offset - field)) - 1.0
    )


def two(x):
    high = x.astype(jnp.bfloat16)
    return high, (x - high.astype(jnp.float32)).astype(jnp.bfloat16)


def three(x):
    high = x.astype(jnp.bfloat16)
    rest = x - high.astype(jnp.float32)
    middle = rest.astype(jnp.bfloat16)
    return high, middle, (rest - middle.astype(jnp.float32)).astype(jnp.bfloat16)


def dot(a, b, dims):
    return lax.dot_general(a, b, dims, preferred_element_type=jnp.float32)


def dot_split(x, high, low, dims):
    rows = x.shape[0]
    x_high, x_low = two(x)
    both = dot(jnp.concatenate([x_high, x_low], axis=0), high, dims)
    return both[:rows] + both[rows:] + dot(x_high, low, dims)


def dot_pick(pick, values, dims):
    parts = [dot(pick, part, dims) for part in three(values)]
    return parts[0] + (parts[1] + parts[2])


def kernel(
    wide_count,
    narrow_count,
    field_ref,
    counts_ref,
    offset_ref,
    kriging_ref,
    whiten_ref,
    near_ref,
    list_ref,
    home_ref,
    coarse_ref,
    coarse_counts_ref,
    coarse_offset_ref,
    coarse_whiten_ref,
    fine_out,
    coarse_out,
    weights,
    weights_high,
    weights_low,
    gain_high,
    gain_low,
    padded,
    rim,
    rim_in,
    own_slices,
    slices,
    picks,
    far_send,
    far_recv,
    far,
    back_near,
    resid,
    back_white,
    terms_send,
    terms_recv,
    sums,
    sums_in,
    totals,
    spots,
    weight_sems,
    sems,
):
    rows_here, cols_here, chains, sites = field_ref.shape
    blocks = rows_here * cols_here
    owned = coarse_ref.shape[0]
    near_count, far_count = near_ref.shape[2], list_ref.shape[2]
    reads = blocks * far_count
    coarse_total = owned * wide_count
    piece = chains // SLICES
    tile = owned * piece
    message = reads * piece
    near_sites = near_count * sites

    w = lax.axis_index("wide")
    n = lax.axis_index("narrow")
    half = lax.rem(w // 8, 2)
    mine = lax.rem(n, 4) + 4 * half

    def sem(i):
        return sems.at[i]

    weight_copies = [
        pltpu.make_async_copy(kriging_ref.at[b], weights.at[b], weight_sems.at[b])
        for b in range(blocks)
    ]
    for copy in weight_copies:
        copy.start()

    for s in range(SLICES):
        for j in range(owned):
            own_slices[s, j * piece : (j + 1) * piece, :] = coarse_ref[
                j, s * piece : (s + 1) * piece, :
            ]

    lane = lax.broadcasted_iota(jnp.int32, (1, coarse_total), 1)
    for i in range(blocks):
        for j in range(far_count):
            number = list_ref[i // cols_here, i % cols_here, j]
            picks[mine, pl.ds(i * far_count + j, 1), :] = (lane == home_ref[number]).astype(
                jnp.float32
            )

    own_rows = pl.ds(pl.multiple_of(w * tile, tile), tile)
    own_copy = pltpu.make_async_copy(own_slices.at[mine], slices.at[own_rows], sem(1))
    own_copy.start()

    def send_slice(t, carry):
        to = lax.rem(w + t, wide_count)
        part = lax.rem(n, 4) + 4 * lax.rem(to // 8, 2)
        pltpu.make_async_remote_copy(
            src_ref=own_slices.at[part],
            dst_ref=slices.at[own_rows],
            send_sem=sem(0),
            recv_sem=sem(1),
            device_id=(to, n),
            device_id_type=MESH,
        ).start()
        return carry

    lax.fori_loop(1, wide_count, send_slice, 0)

    core, pair, quad = lax.rem(n, 2), lax.rem(n // 2, 2), n // 4
    members = []
    for t in range(1, GROUP):
        c = 1 - core if t % 2 else core
        p = 1 - pair if (t // 2) % 2 else pair
        h = 1 - half if t // 4 else half
        members.append((w + 8 * (h - half), quad * 4 + p * 2 + c, c + 2 * p + 4 * h))

    for to_w, to_n, _ in members:
        pltpu.make_async_remote_copy(
            src_ref=picks.at[mine],
            dst_ref=picks.at[mine],
            send_sem=sem(2),
            recv_sem=sem(3),
            device_id=(to_w, to_n),
            device_id_type=MESH,
        ).start()

    up, down = lax.rem(w + 1, wide_count), lax.rem(w + wide_count - 1, wide_count)
    right, left = lax.rem(n + 1, narrow_count), lax.rem(n + narrow_count - 1, narrow_count)
    last_r, last_c = rows_here, cols_here
    row_spans = {-1: (pl.ds(1, 1), down), 0: (pl.ds(1, rows_here), w), 1: (pl.ds(last_r, 1), up)}
    col_spans = {-1: (pl.ds(1, 1), left), 0: (pl.ds(1, cols_here), n), 1: (pl.ds(last_c, 1), right)}
    rim_rows = {-1: pl.ds(0, 1), 0: pl.ds(1, rows_here), 1: pl.ds(last_r + 1, 1)}
    rim_cols = {-1: pl.ds(0, 1), 0: pl.ds(1, cols_here), 1: pl.ds(last_c + 1, 1)}
    for r in range(rows_here):
        for c in range(cols_here):
            padded[r + 1, c + 1] = field_ref[r, c]
    for dr, dc in PLACES:
        (from_r, to_w), (from_c, to_n) = row_spans[dr], col_spans[dc]
        pltpu.make_async_remote_copy(
            src_ref=padded.at[from_r, from_c],
            dst_ref=padded.at[rim_rows[-dr], rim_cols[-dc]],
            send_sem=sem(4),
            recv_sem=sem(5),
            device_id=(to_w, to_n),
            device_id_type=MESH,
        ).start()

    for b in range(blocks):
        r, c = b // cols_here, b % cols_here
        for k in range(near_count):
            number = near_ref[r, c, k]
            grid_cols = cols_here * narrow_count
            row = number // grid_cols - w * rows_here + 1
            row = jnp.where(row < 0, row + rows_here * wide_count, row)
            row = jnp.where(row > rows_here + 1, row - rows_here * wide_count, row)
            col = lax.rem(number, grid_cols) - n * cols_here + 1
            col = jnp.where(col < 0, col + grid_cols, col)
            col = jnp.where(col > cols_here + 1, col - grid_cols, col)
            row, col = jnp.clip(row, 0, rows_here + 1), jnp.clip(col, 0, cols_here + 1)
            spots[b * near_count + k] = row * (cols_here + 2) + col

    for b in range(blocks):
        gain = lax.dot_general(
            whiten_ref[b], whiten_ref[b], TN, precision=EXACT, preferred_element_type=jnp.float32
        )
        gain_high[b], gain_low[b] = two(gain)
    for j in range(owned):
        white = lax.dot_general(
            coarse_ref[j], coarse_whiten_ref[j], NT, precision=EXACT,
            preferred_element_type=jnp.float32,
        )
        prior = lax.dot_general(
            white, coarse_whiten_ref[j], NN, precision=EXACT, preferred_element_type=jnp.float32
        )
        coarse_out[j] = (
            weibull(coarse_ref[j], coarse_counts_ref[j : j + 1, :], coarse_offset_ref[j : j + 1, :])
            - prior
        )
    for b in range(blocks):
        r, c = b // cols_here, b % cols_here
        fine_out[r, c] = weibull(
            field_ref[r, c], counts_ref[b : b + 1, :], offset_ref[b : b + 1, :]
        )
        weight_copies[b].wait()
        weights_high[b], weights_low[b] = two(weights[b])
        back_near[b, near_count] = jnp.zeros((chains, sites), jnp.float32)

    pltpu.make_async_copy(slices, slices, sem(1)).wait()
    other_picks = picks.at[pl.ds(0, GROUP - 1)]
    pltpu.make_async_copy(other_picks, other_picks, sem(3)).wait()
    held = jnp.concatenate(
        [slices[pl.ds(r, coarse_total, stride=piece), :] for r in range(piece)], axis=1
    )
    pick = jnp.concatenate([picks[s] for s in range(GROUP)], axis=0).astype(jnp.bfloat16)
    chosen = dot_pick(pick, held, NN)
    for r in range(piece):
        far_send[pl.ds(r, GROUP * reads, stride=piece), :] = chosen[:, r * sites : (r + 1) * sites]

    def group_rows(s):
        return pl.ds(pl.multiple_of(s * message, message), message)

    def exchange(source, target, send_sem, recv_sem):
        pltpu.make_async_copy(
            source.at[group_rows(mine)], target.at[group_rows(mine)], recv_sem
        ).start()
        for to_w, to_n, s in members:
            pltpu.make_async_remote_copy(
                src_ref=source.at[group_rows(s)],
                dst_ref=target.at[group_rows(mine)],
                send_sem=send_sem,
                recv_sem=recv_sem,
                device_id=(to_w, to_n),
                device_id_type=MESH,
            ).start()

    exchange(far_send, far_recv, sem(6), sem(7))

    interior = padded.at[pl.ds(0, 4)]
    pltpu.make_async_copy(interior, interior, sem(5)).wait()
    width = cols_here + 2
    for b in range(blocks):
        r, c = b // cols_here, b % cols_here
        fields = []
        for k in range(near_count):
            spot = spots[b * near_count + k]
            fields.append(padded[spot // width, lax.rem(spot, width)])
        near = jnp.concatenate(fields, axis=1)
        resid[b] = field_ref[r, c] - dot_split(
            near, weights_high[b, :, :near_sites], weights_low[b, :, :near_sites], NT
        )

    pltpu.make_async_copy(far_recv, far_recv, sem(7)).wait()
    for s in range(SLICES):
        for i in range(reads):
            far[i, s * piece : (s + 1) * piece, :] = far_recv[
                s * message + i * piece : s * message + (i + 1) * piece, :
            ]
    for b in range(blocks):
        distant = jnp.concatenate([far[b * far_count + j] for j in range(far_count)], axis=1)
        left_over = resid[b] - dot_split(
            distant, weights_high[b, :, near_sites:], weights_low[b, :, near_sites:], NT
        )
        back_white[b] = dot_split(left_over, gain_high[b], gain_low[b], NN)
    for b in range(blocks):
        back = dot_split(
            back_white[b], weights_high[b, :, near_sites:], weights_low[b, :, near_sites:], NN
        )
        for j in range(far_count):
            i = b * far_count + j
            for s in range(SLICES):
                terms_send[s * message + i * piece : s * message + (i + 1) * piece, :] = back[
                    s * piece : (s + 1) * piece, j * sites : (j + 1) * sites
                ]
    exchange(terms_send, terms_recv, sem(8), sem(9))

    for b in range(blocks):
        back = dot_split(
            back_white[b], weights_high[b, :, :near_sites], weights_low[b, :, :near_sites], NN
        )
        for k in range(near_count):
            back_near[b, k] = back[:, k * sites : (k + 1) * sites]
    for pr in range(rows_here + 2):
        for pc in range(cols_here + 2):
            total = None
            for b in range(blocks):
                r, c = b // cols_here + 1, b % cols_here + 1
                if max(abs(r - pr), abs(c - pc)) != 1:
                    continue
                slot = jnp.int32(near_count)
                for k in range(near_count):
                    slot = jnp.where(
                        spots[b * near_count + k] == pr * width + pc, jnp.int32(k), slot
                    )
                term = back_near[b, slot]
                total = term if total is None else total + term
            rim[pr, pc] = total
    for dr, dc in PLACES:
        to_w, to_n = row_spans[dr][1], col_spans[dc][1]
        pltpu.make_async_remote_copy(
            src_ref=rim.at[rim_rows[dr], rim_cols[dc]],
            dst_ref=rim_in.at[rim_rows[-dr], rim_cols[-dc]],
            send_sem=sem(10),
            recv_sem=sem(11),
            device_id=(to_w, to_n),
            device_id_type=MESH,
        ).start()

    pltpu.make_async_copy(terms_recv, terms_recv, sem(9)).wait()
    gathered = jnp.concatenate(
        [terms_recv[pl.ds(r, GROUP * reads, stride=piece), :] for r in range(piece)], axis=1
    )
    summed = dot_pick(pick, gathered, TN)
    for r in range(piece):
        sums[pl.ds(r, coarse_total, stride=piece), :] = summed[:, r * sites : (r + 1) * sites]
    place = (w // 16 * 8 + lax.rem(w, 8)) * 2 + quad

    def send_sum(to):
        rows = pl.ds(pl.multiple_of(to * tile, tile), tile)
        return pltpu.make_async_remote_copy(
            src_ref=sums.at[rows],
            dst_ref=sums_in.at[place],
            send_sem=sem(12),
            recv_sem=sem(13),
            device_id=(to, mine),
            device_id_type=MESH,
        )

    def send_sums(t, carry):
        send_sum(lax.rem(w + t, wide_count)).start()
        return carry

    lax.fori_loop(1, wide_count, send_sums, 0)

    @pl.when(mine == n)
    def _():
        pltpu.make_async_copy(sums.at[own_rows], sums_in.at[place], sem(13)).start()

    @pl.when(mine != n)
    def _():
        send_sum(w).start()

    around = rim_in.at[pl.ds(0, 4)]
    pltpu.make_async_copy(around, around, sem(11)).wait()
    for r in range(rows_here):
        for c in range(cols_here):
            total = fine_out[r, c] - back_white[r * cols_here + c] + rim[r + 1, c + 1]
            edge_r = [e for e, at in ((0, 0), (last_r + 1, rows_here - 1)) if r == at]
            edge_c = [e for e, at in ((0, 0), (last_c + 1, cols_here - 1)) if c == at]
            for e in edge_r:
                total = total + rim_in[e, c + 1]
            for f in edge_c:
                total = total + rim_in[r + 1, f]
            for e in edge_r:
                for f in edge_c:
                    total = total + rim_in[e, f]
            fine_out[r, c] = total

    pltpu.make_async_copy(sums_in, sums_in, sem(13)).wait()
    totals[n] = jnp.sum(sums_in[...], axis=0)
    for t in range(1, narrow_count):
        pltpu.make_async_remote_copy(
            src_ref=totals.at[n],
            dst_ref=totals.at[n],
            send_sem=sem(14),
            recv_sem=sem(15),
            device_id=(w, lax.rem(n + t, narrow_count)),
            device_id_type=MESH,
        ).start()
    other_totals = totals.at[pl.ds(0, narrow_count - 1)]
    pltpu.make_async_copy(other_totals, other_totals, sem(15)).wait()
    for s in range(SLICES):
        for j in range(owned):
            rows = slice(s * piece, (s + 1) * piece)
            coarse_out[j, rows, :] = (
                coarse_out[j, rows, :] + totals[s, j * piece : (j + 1) * piece, :]
            )

    sent = slices.at[pl.ds(0, (wide_count - 1) * tile)]
    pltpu.make_async_copy(sent, sent, sem(0)).wait()
    pltpu.make_async_copy(other_picks, other_picks, sem(2)).wait()
    pltpu.make_async_copy(interior, interior, sem(4)).wait()
    others = far_send.at[pl.ds(0, (GROUP - 1) * message)]
    pltpu.make_async_copy(others, others, sem(6)).wait()
    pltpu.make_async_copy(others, others, sem(8)).wait()
    pltpu.make_async_copy(around, around, sem(10)).wait()
    pltpu.make_async_copy(sent, sent, sem(12)).wait()

    @pl.when(mine != n)
    def _():
        one = sums.at[pl.ds(0, tile)]
        pltpu.make_async_copy(one, one, sem(12)).wait()

    pltpu.make_async_copy(other_totals, other_totals, sem(14)).wait()


def per_device(
    wide_count,
    narrow_count,
    fine_field,
    fine_counts,
    fine_offset,
    kriging,
    whiten,
    neighbours,
    coarse_list,
    coarse_field,
    coarse_counts,
    coarse_offset,
    coarse_whiten,
    coarse_home,
):
    rows_here, cols_here, chains, sites = fine_field.shape
    blocks = rows_here * cols_here
    owned = coarse_field.shape[0]
    cond = kriging.shape[3]
    near_count, far_count = neighbours.shape[2], coarse_list.shape[2]
    reads = blocks * far_count
    piece = chains // SLICES
    f32, bf16 = jnp.float32, jnp.bfloat16
    vmem = pl.BlockSpec(memory_space=pltpu.VMEM)
    smem = pl.BlockSpec(memory_space=pltpu.SMEM)
    return pl.pallas_call(
        functools.partial(kernel, wide_count, narrow_count),
        out_shape=(
            jax.ShapeDtypeStruct(fine_field.shape, f32),
            jax.ShapeDtypeStruct(coarse_field.shape, f32),
        ),
        in_specs=[vmem, vmem, vmem, pl.BlockSpec(memory_space=pl.ANY), vmem, smem, smem, smem]
        + [vmem] * 4,
        out_specs=(vmem, vmem),
        scratch_shapes=[
            pltpu.VMEM((blocks, sites, cond), f32),
            pltpu.VMEM((blocks, sites, cond), bf16),
            pltpu.VMEM((blocks, sites, cond), bf16),
            pltpu.VMEM((blocks, sites, sites), bf16),
            pltpu.VMEM((blocks, sites, sites), bf16),
            pltpu.VMEM((rows_here + 2, cols_here + 2, chains, sites), f32),
            pltpu.VMEM((rows_here + 2, cols_here + 2, chains, sites), f32),
            pltpu.VMEM((rows_here + 2, cols_here + 2, chains, sites), f32),
            pltpu.VMEM((SLICES, owned * piece, sites), f32),
            pltpu.VMEM((wide_count * owned * piece, sites), f32),
            pltpu.VMEM((GROUP, reads, wide_count * owned), f32),
            pltpu.VMEM((GROUP * reads * piece, sites), f32),
            pltpu.VMEM((GROUP * reads * piece, sites), f32),
            pltpu.VMEM((reads, chains, sites), f32),
            pltpu.VMEM((blocks, near_count + 1, chains, sites), f32),
            pltpu.VMEM((blocks, chains, sites), f32),
            pltpu.VMEM((blocks, chains, sites), f32),
            pltpu.VMEM((GROUP * reads * piece, sites), f32),
            pltpu.VMEM((GROUP * reads * piece, sites), f32),
            pltpu.VMEM((wide_count * owned * piece, sites), f32),
            pltpu.VMEM((wide_count, owned * piece, sites), f32),
            pltpu.VMEM((narrow_count, owned * piece, sites), f32),
            pltpu.SMEM((blocks * near_count,), jnp.int32),
            pltpu.SemaphoreType.DMA((blocks,)),
            pltpu.SemaphoreType.DMA((16,)),
        ],
        compiler_params=pltpu.CompilerParams(
            has_side_effects=True, vmem_limit_bytes=60 * 1024 * 1024
        ),
    )(
        fine_field,
        fine_counts.reshape(blocks, sites),
        fine_offset.reshape(blocks, sites),
        kriging.reshape(blocks, sites, cond),
        whiten.reshape(blocks, sites, sites),
        neighbours,
        coarse_list,
        coarse_home,
        coarse_field,
        coarse_counts,
        coarse_offset,
        coarse_whiten,
    )


def solution(mesh):
    return jax.shard_map(
        functools.partial(per_device, mesh.shape["wide"], mesh.shape["narrow"]),
        mesh=mesh,
        in_specs=(
            P("wide", "narrow", None, None),
            P("wide", "narrow", None),
            P("wide", "narrow", None),
            P("wide", "narrow", None, None),
            P("wide", "narrow", None, None),
            P("wide", "narrow", None),
            P("wide", "narrow", None),
            P("wide", None, None),
            P("wide", None),
            P("wide", None),
            P("wide", None, None),
            P(),
        ),
        out_specs=(P("wide", "narrow", None, None), P("wide", None, None)),
        check_vma=False,
    )
```

```python
import functools

import jax
import jax.numpy as jnp
from jax import lax
from jax.experimental import pallas as pl
from jax.experimental.pallas import tpu as pltpu
from jax.sharding import PartitionSpec as P

SHAPE_K = 1.25
EXACT = lax.Precision.HIGHEST
MESH = pl.DeviceIdType.MESH
NT = (((1,), (1,)), ((), ()))
NN = (((1,), (0,)), ((), ()))
TN = (((0,), (0,)), ((), ()))
PLACES = ((-1, -1), (-1, 0), (-1, 1), (0, -1), (0, 1), (1, -1), (1, 0), (1, 1))

RUN = 4
SLICES = 8
GROUP = 8


def weibull(field, counts, offset):
    return SHAPE_K * (
        jnp.exp(SHAPE_K * (jnp.log(counts.astype(jnp.float32)) - offset - field)) - 1.0
    )


def two(x):
    high = x.astype(jnp.bfloat16)
    return high, (x - high.astype(jnp.float32)).astype(jnp.bfloat16)


def three(x):
    high = x.astype(jnp.bfloat16)
    rest = x - high.astype(jnp.float32)
    middle = rest.astype(jnp.bfloat16)
    return high, middle, (rest - middle.astype(jnp.float32)).astype(jnp.bfloat16)


def dot(a, b, dims):
    return lax.dot_general(a, b, dims, preferred_element_type=jnp.float32)


def dot_split(x, high, low, dims):
    rows = x.shape[0]
    x_high, x_low = two(x)
    both = dot(jnp.concatenate([x_high, x_low], axis=0), high, dims)
    return both[:rows] + both[rows:] + dot(x_high, low, dims)


def dot_pick(pick, values, dims):
    parts = [dot(pick, part, dims) for part in three(values)]
    return parts[0] + (parts[1] + parts[2])


def kernel(
    wide_count,
    narrow_count,
    kriging_ref,
    *refs,
):
    inputs, (fine_out, coarse_out), held_here = refs[:11], refs[11:13], refs[13:24]
    (
        field_ref,
        counts_ref,
        offset_ref,
        whiten_ref,
        near_ref,
        list_ref,
        home_ref,
        coarse_ref,
        coarse_counts_ref,
        coarse_offset_ref,
        coarse_whiten_ref,
    ) = held_here
    (
        weights,
        weights_high,
        weights_low,
        gain_high,
        gain_low,
        padded,
        rim,
        rim_in,
        own_slices,
        slices,
        picks,
        far_send,
        far_recv,
        far,
        back_near,
        resid,
        back_white,
        terms_send,
        terms_recv,
        sums,
        sums_beside,
        plane_sums,
        sums_in,
        totals,
        spots,
        weight_sems,
        sems,
        copy_sems,
    ) = refs[24:]
    rows_here, cols_here, chains, sites = field_ref.shape
    blocks = rows_here * cols_here
    owned = coarse_ref.shape[0]
    near_count, far_count = near_ref.shape[2], list_ref.shape[0]
    reads = blocks * far_count
    coarse_total = owned * wide_count
    piece = chains // SLICES
    tile = owned * piece
    message = reads * piece
    near_sites = near_count * sites

    w = lax.axis_index("wide")
    n = lax.axis_index("narrow")
    half = lax.rem(w // 8, 2)
    mine = lax.rem(n, 4) + 4 * half
    planes = wide_count // RUN
    x, plane = lax.rem(w, RUN), w // RUN
    place = x * planes + plane

    def sem(i):
        return sems.at[i]

    copies = {}
    for i in (7, 4, 5, 6, 0, 1, 2, 8, 9, 10, 3):
        copies[i] = pltpu.make_async_copy(inputs[i], held_here[i], copy_sems.at[i])
        copies[i].start()
    weight_copies = [
        pltpu.make_async_copy(kriging_ref.at[b], weights.at[b], weight_sems.at[b])
        for b in range(blocks)
    ]
    for copy in weight_copies:
        copy.start()

    core, pair, quad = lax.rem(n, 2), lax.rem(n // 2, 2), n // 4
    members = []
    for t in range(1, GROUP):
        c = 1 - core if t % 2 else core
        p = 1 - pair if (t // 2) % 2 else pair
        h = 1 - half if t // 4 else half
        members.append((w + 8 * (h - half), quad * 4 + p * 2 + c, c + 2 * p + 4 * h))
    up, down = lax.rem(w + 1, wide_count), lax.rem(w + wide_count - 1, wide_count)
    right, left = lax.rem(n + 1, narrow_count), lax.rem(n + narrow_count - 1, narrow_count)

    barrier = pltpu.get_barrier_semaphore()

    def greet(to_w, to_n):
        pl.semaphore_signal(barrier, inc=1, device_id=(to_w, to_n), device_id_type=MESH)

    def across(t):
        return lax.rem(plane + t, planes)

    def beside(t):
        return lax.rem(x + t, RUN)

    def greet_planes(t, carry):
        greet(across(t) * RUN + x, n)
        return carry

    lax.fori_loop(1, planes, greet_planes, 0)
    for t in range(1, RUN):
        greet(plane * RUN + beside(t), n)
    for t in range(1, narrow_count):
        greet(w, lax.rem(n + t, narrow_count))
    for to_w, to_n, _ in members[4:]:
        greet(to_w, to_n)
    for to_w in (up, down):
        for to_n in (left, n, right):
            greet(to_w, to_n)
    greetings = planes - 1 + RUN - 1 + narrow_count - 1 + 3 + 6

    copies[7].wait()
    for s in range(SLICES):
        for j in range(owned):
            own_slices[s, j * piece : (j + 1) * piece, :] = coarse_ref[
                j, s * piece : (s + 1) * piece, :
            ]

    copies[5].wait()
    copies[6].wait()
    lane = lax.broadcasted_iota(jnp.int32, (1, coarse_total), 1)
    for i in range(blocks):
        for j in range(far_count):
            number = list_ref[j, i % cols_here, i // cols_here]
            owner, which = home_ref[number] // owned, lax.rem(home_ref[number], owned)
            column = (lax.rem(owner, RUN) * planes + owner // RUN) * owned + which
            picks[mine, pl.ds(i * far_count + j, 1), :] = (lane == column).astype(jnp.float32)

    copies[0].wait()
    for r in range(rows_here):
        for c in range(cols_here):
            padded[r + 1, c + 1] = field_ref[r, c]

    pl.semaphore_wait(barrier, greetings)
    own_rows = pl.ds(pl.multiple_of(place * tile, tile), tile)
    own_copy = pltpu.make_async_copy(own_slices.at[mine], slices.at[own_rows], sem(1))
    own_copy.start()

    def send_slice(t, carry):
        to = across(t) * RUN + x
        part = lax.rem(n, 4) + 4 * lax.rem(to // 8, 2)
        pltpu.make_async_remote_copy(
            src_ref=own_slices.at[part],
            dst_ref=slices.at[own_rows],
            send_sem=sem(0),
            recv_sem=sem(1),
            device_id=(to, n),
            device_id_type=MESH,
        ).start()
        return carry

    lax.fori_loop(1, planes, send_slice, 0)

    for to_w, to_n, _ in members:
        pltpu.make_async_remote_copy(
            src_ref=picks.at[mine],
            dst_ref=picks.at[mine],
            send_sem=sem(2),
            recv_sem=sem(3),
            device_id=(to_w, to_n),
            device_id_type=MESH,
        ).start()

    last_r, last_c = rows_here, cols_here
    row_spans = {-1: (pl.ds(1, 1), down), 0: (pl.ds(1, rows_here), w), 1: (pl.ds(last_r, 1), up)}
    col_spans = {-1: (pl.ds(1, 1), left), 0: (pl.ds(1, cols_here), n), 1: (pl.ds(last_c, 1), right)}
    rim_rows = {-1: pl.ds(0, 1), 0: pl.ds(1, rows_here), 1: pl.ds(last_r + 1, 1)}
    rim_cols = {-1: pl.ds(0, 1), 0: pl.ds(1, cols_here), 1: pl.ds(last_c + 1, 1)}
    for dr, dc in PLACES:
        (from_r, to_w), (from_c, to_n) = row_spans[dr], col_spans[dc]
        pltpu.make_async_remote_copy(
            src_ref=padded.at[from_r, from_c],
            dst_ref=padded.at[rim_rows[-dr], rim_cols[-dc]],
            send_sem=sem(4),
            recv_sem=sem(5),
            device_id=(to_w, to_n),
            device_id_type=MESH,
        ).start()

    def run_rows(at):
        return pl.ds(pl.multiple_of(at * planes * tile, planes * tile), planes * tile)

    gathered_here = slices.at[run_rows(x)]
    pltpu.make_async_copy(gathered_here, gathered_here, sem(1)).wait()
    for t in range(1, RUN):
        pltpu.make_async_remote_copy(
            src_ref=gathered_here,
            dst_ref=gathered_here,
            send_sem=sem(16),
            recv_sem=sem(17),
            device_id=(plane * RUN + beside(t), n),
            device_id_type=MESH,
        ).start()
    other_runs = slices.at[pl.ds(0, (RUN - 1) * planes * tile)]

    copies[4].wait()
    for b in range(blocks):
        r, c = b // cols_here, b % cols_here
        for k in range(near_count):
            number = near_ref[r, c, k]
            grid_cols = cols_here * narrow_count
            row = number // grid_cols - w * rows_here + 1
            row = jnp.where(row < 0, row + rows_here * wide_count, row)
            row = jnp.where(row > rows_here + 1, row - rows_here * wide_count, row)
            col = lax.rem(number, grid_cols) - n * cols_here + 1
            col = jnp.where(col < 0, col + grid_cols, col)
            col = jnp.where(col > cols_here + 1, col - grid_cols, col)
            row, col = jnp.clip(row, 0, rows_here + 1), jnp.clip(col, 0, cols_here + 1)
            spots[b * near_count + k] = row * (cols_here + 2) + col

    for i in (1, 2, 3, 8, 9, 10):
        copies[i].wait()
    for b in range(blocks):
        gain = lax.dot_general(
            whiten_ref[b], whiten_ref[b], TN, precision=EXACT, preferred_element_type=jnp.float32
        )
        gain_high[b], gain_low[b] = two(gain)
    for j in range(owned):
        white = lax.dot_general(
            coarse_ref[j], coarse_whiten_ref[j], NT, precision=EXACT,
            preferred_element_type=jnp.float32,
        )
        prior = lax.dot_general(
            white, coarse_whiten_ref[j], NN, precision=EXACT, preferred_element_type=jnp.float32
        )
        coarse_out[j] = (
            weibull(coarse_ref[j], coarse_counts_ref[j : j + 1, :], coarse_offset_ref[j : j + 1, :])
            - prior
        )
    for b in range(blocks):
        r, c = b // cols_here, b % cols_here
        fine_out[r, c] = weibull(
            field_ref[r, c], counts_ref[b : b + 1, :], offset_ref[b : b + 1, :]
        )
        weight_copies[b].wait()
        weights_high[b], weights_low[b] = two(weights[b])
        back_near[b, near_count] = jnp.zeros((chains, sites), jnp.float32)

    pltpu.make_async_copy(other_runs, other_runs, sem(17)).wait()
    other_picks = picks.at[pl.ds(0, GROUP - 1)]
    pltpu.make_async_copy(other_picks, other_picks, sem(3)).wait()
    held = jnp.concatenate(
        [slices[pl.ds(r, coarse_total, stride=piece), :] for r in range(piece)], axis=1
    )
    pick = jnp.concatenate([picks[s] for s in range(GROUP)], axis=0).astype(jnp.bfloat16)
    chosen = dot_pick(pick, held, NN)
    for r in range(piece):
        far_send[pl.ds(r, GROUP * reads, stride=piece), :] = chosen[:, r * sites : (r + 1) * sites]

    def group_rows(s):
        return pl.ds(pl.multiple_of(s * message, message), message)

    def exchange(source, target, send_sem, recv_sem):
        pltpu.make_async_copy(
            source.at[group_rows(mine)], target.at[group_rows(mine)], recv_sem
        ).start()
        for to_w, to_n, s in members:
            pltpu.make_async_remote_copy(
                src_ref=source.at[group_rows(s)],
                dst_ref=target.at[group_rows(mine)],
                send_sem=send_sem,
                recv_sem=recv_sem,
                device_id=(to_w, to_n),
                device_id_type=MESH,
            ).start()

    exchange(far_send, far_recv, sem(6), sem(7))

    interior = padded.at[pl.ds(0, 4)]
    pltpu.make_async_copy(interior, interior, sem(5)).wait()
    width = cols_here + 2
    for b in range(blocks):
        r, c = b // cols_here, b % cols_here
        fields = []
        for k in range(near_count):
            spot = spots[b * near_count + k]
            fields.append(padded[spot // width, lax.rem(spot, width)])
        near = jnp.concatenate(fields, axis=1)
        resid[b] = field_ref[r, c] - dot_split(
            near, weights_high[b, :, :near_sites], weights_low[b, :, :near_sites], NT
        )

    pltpu.make_async_copy(far_recv, far_recv, sem(7)).wait()
    for s in range(SLICES):
        for i in range(reads):
            far[i, s * piece : (s + 1) * piece, :] = far_recv[
                s * message + i * piece : s * message + (i + 1) * piece, :
            ]
    for b in range(blocks):
        distant = jnp.concatenate([far[b * far_count + j] for j in range(far_count)], axis=1)
        left_over = resid[b] - dot_split(
            distant, weights_high[b, :, near_sites:], weights_low[b, :, near_sites:], NT
        )
        back_white[b] = dot_split(left_over, gain_high[b], gain_low[b], NN)
    for b in range(blocks):
        back = dot_split(
            back_white[b], weights_high[b, :, near_sites:], weights_low[b, :, near_sites:], NN
        )
        for j in range(far_count):
            i = b * far_count + j
            for s in range(SLICES):
                terms_send[s * message + i * piece : s * message + (i + 1) * piece, :] = back[
                    s * piece : (s + 1) * piece, j * sites : (j + 1) * sites
                ]
    exchange(terms_send, terms_recv, sem(8), sem(9))

    for b in range(blocks):
        back = dot_split(
            back_white[b], weights_high[b, :, :near_sites], weights_low[b, :, :near_sites], NN
        )
        for k in range(near_count):
            back_near[b, k] = back[:, k * sites : (k + 1) * sites]
    for pr in range(rows_here + 2):
        for pc in range(cols_here + 2):
            total = None
            for b in range(blocks):
                r, c = b // cols_here + 1, b % cols_here + 1
                if max(abs(r - pr), abs(c - pc)) != 1:
                    continue
                slot = jnp.int32(near_count)
                for k in range(near_count):
                    slot = jnp.where(
                        spots[b * near_count + k] == pr * width + pc, jnp.int32(k), slot
                    )
                term = back_near[b, slot]
                total = term if total is None else total + term
            rim[pr, pc] = total
    for dr, dc in PLACES:
        to_w, to_n = row_spans[dr][1], col_spans[dc][1]
        pltpu.make_async_remote_copy(
            src_ref=rim.at[rim_rows[dr], rim_cols[dc]],
            dst_ref=rim_in.at[rim_rows[-dr], rim_cols[-dc]],
            send_sem=sem(10),
            recv_sem=sem(11),
            device_id=(to_w, to_n),
            device_id_type=MESH,
        ).start()

    pltpu.make_async_copy(terms_recv, terms_recv, sem(9)).wait()
    gathered = jnp.concatenate(
        [terms_recv[pl.ds(r, GROUP * reads, stride=piece), :] for r in range(piece)], axis=1
    )
    summed = dot_pick(pick, gathered, TN)
    for r in range(piece):
        sums[pl.ds(r, coarse_total, stride=piece), :] = summed[:, r * sites : (r + 1) * sites]

    pltpu.make_async_copy(sums.at[run_rows(x)], sums_beside.at[x], sem(19)).start()
    for t in range(1, RUN):
        pltpu.make_async_remote_copy(
            src_ref=sums.at[run_rows(beside(t))],
            dst_ref=sums_beside.at[x],
            send_sem=sem(18),
            recv_sem=sem(19),
            device_id=(plane * RUN + beside(t), n),
            device_id_type=MESH,
        ).start()
    pltpu.make_async_copy(sums_beside, sums_beside, sem(19)).wait()
    plane_sums[...] = jnp.sum(sums_beside[...], axis=0).reshape(planes, tile, sites)
    pltpu.make_async_copy(plane_sums.at[plane], sums_in.at[plane], sem(13)).start()

    def send_sums(t, carry):
        pltpu.make_async_remote_copy(
            src_ref=plane_sums.at[across(t)],
            dst_ref=sums_in.at[plane],
            send_sem=sem(12),
            recv_sem=sem(13),
            device_id=(across(t) * RUN + x, n),
            device_id_type=MESH,
        ).start()
        return carry

    lax.fori_loop(1, planes, send_sums, 0)

    around = rim_in.at[pl.ds(0, 4)]
    pltpu.make_async_copy(around, around, sem(11)).wait()
    for r in range(rows_here):
        for c in range(cols_here):
            total = fine_out[r, c] - back_white[r * cols_here + c] + rim[r + 1, c + 1]
            edge_r = [e for e, at in ((0, 0), (last_r + 1, rows_here - 1)) if r == at]
            edge_c = [e for e, at in ((0, 0), (last_c + 1, cols_here - 1)) if c == at]
            for e in edge_r:
                total = total + rim_in[e, c + 1]
            for f in edge_c:
                total = total + rim_in[r + 1, f]
            for e in edge_r:
                for f in edge_c:
                    total = total + rim_in[e, f]
            fine_out[r, c] = total

    pltpu.make_async_copy(sums_in, sums_in, sem(13)).wait()
    totals[n] = jnp.sum(
        sums_in[...].reshape(planes // 4, 2, 2, tile, sites), axis=(0, 2)
    )
    for t in range(1, narrow_count):
        pltpu.make_async_remote_copy(
            src_ref=totals.at[n],
            dst_ref=totals.at[n],
            send_sem=sem(14),
            recv_sem=sem(15),
            device_id=(w, lax.rem(n + t, narrow_count)),
            device_id_type=MESH,
        ).start()
    other_totals = totals.at[pl.ds(0, narrow_count - 1)]
    pltpu.make_async_copy(other_totals, other_totals, sem(15)).wait()
    for s in range(SLICES):
        for j in range(owned):
            rows = slice(s * piece, (s + 1) * piece)
            coarse_out[j, rows, :] = (
                coarse_out[j, rows, :]
                + totals[s % 4, s // 4, j * piece : (j + 1) * piece, :]
                + totals[s % 4 + 4, s // 4, j * piece : (j + 1) * piece, :]
            )

    sent = sums_in.at[pl.ds(0, planes - 1)]
    pltpu.make_async_copy(sent, sent, sem(0)).wait()
    pltpu.make_async_copy(other_runs, other_runs, sem(16)).wait()
    pltpu.make_async_copy(other_runs, other_runs, sem(18)).wait()
    pltpu.make_async_copy(other_picks, other_picks, sem(2)).wait()
    pltpu.make_async_copy(interior, interior, sem(4)).wait()
    others = far_send.at[pl.ds(0, (GROUP - 1) * message)]
    pltpu.make_async_copy(others, others, sem(6)).wait()
    pltpu.make_async_copy(others, others, sem(8)).wait()
    pltpu.make_async_copy(around, around, sem(10)).wait()
    pltpu.make_async_copy(sent, sent, sem(12)).wait()

    pltpu.make_async_copy(other_totals, other_totals, sem(14)).wait()


def per_device(
    wide_count,
    narrow_count,
    fine_field,
    fine_counts,
    fine_offset,
    kriging,
    whiten,
    neighbours,
    coarse_list,
    coarse_field,
    coarse_counts,
    coarse_offset,
    coarse_whiten,
    coarse_home,
):
    rows_here, cols_here, chains, sites = fine_field.shape
    blocks = rows_here * cols_here
    owned = coarse_field.shape[0]
    cond = kriging.shape[3]
    near_count, far_count = neighbours.shape[2], coarse_list.shape[2]
    reads = blocks * far_count
    piece = chains // SLICES
    f32, bf16 = jnp.float32, jnp.bfloat16
    vmem = pl.BlockSpec(memory_space=pltpu.VMEM)
    operands = (
        fine_field,
        fine_counts.reshape(blocks, sites),
        fine_offset.reshape(blocks, sites),
        whiten.reshape(blocks, sites, sites),
        neighbours,
        coarse_list.transpose(2, 1, 0),
        coarse_home,
        coarse_field,
        coarse_counts,
        coarse_offset,
        coarse_whiten,
    )
    return pl.pallas_call(
        functools.partial(kernel, wide_count, narrow_count),
        out_shape=(
            pltpu.VMEM(fine_field.shape, f32),
            pltpu.VMEM(coarse_field.shape, f32),
        ),
        in_specs=[pl.BlockSpec(memory_space=pltpu.HBM)] * (1 + len(operands)),
        out_specs=(vmem, vmem),
        scratch_shapes=[
            (pltpu.SMEM if i in (4, 5, 6) else pltpu.VMEM)(x.shape, x.dtype)
            for i, x in enumerate(operands)
        ]
        + [
            pltpu.VMEM((blocks, sites, cond), f32),
            pltpu.VMEM((blocks, sites, cond), bf16),
            pltpu.VMEM((blocks, sites, cond), bf16),
            pltpu.VMEM((blocks, sites, sites), bf16),
            pltpu.VMEM((blocks, sites, sites), bf16),
            pltpu.VMEM((rows_here + 2, cols_here + 2, chains, sites), f32),
            pltpu.VMEM((rows_here + 2, cols_here + 2, chains, sites), f32),
            pltpu.VMEM((rows_here + 2, cols_here + 2, chains, sites), f32),
            pltpu.VMEM((SLICES, owned * piece, sites), f32),
            pltpu.VMEM((wide_count * owned * piece, sites), f32),
            pltpu.VMEM((GROUP, reads, wide_count * owned), f32),
            pltpu.VMEM((GROUP * reads * piece, sites), f32),
            pltpu.VMEM((GROUP * reads * piece, sites), f32),
            pltpu.VMEM((reads, chains, sites), f32),
            pltpu.VMEM((blocks, near_count + 1, chains, sites), f32),
            pltpu.VMEM((blocks, chains, sites), f32),
            pltpu.VMEM((blocks, chains, sites), f32),
            pltpu.VMEM((GROUP * reads * piece, sites), f32),
            pltpu.VMEM((GROUP * reads * piece, sites), f32),
            pltpu.VMEM((wide_count * owned * piece, sites), f32),
            pltpu.VMEM((RUN, wide_count // RUN * owned * piece, sites), f32),
            pltpu.VMEM((wide_count // RUN, owned * piece, sites), f32),
            pltpu.VMEM((wide_count // RUN, owned * piece, sites), f32),
            pltpu.VMEM((narrow_count, 2, owned * piece, sites), f32),
            pltpu.SMEM((blocks * near_count,), jnp.int32),
            pltpu.SemaphoreType.DMA((blocks,)),
            pltpu.SemaphoreType.DMA((20,)),
            pltpu.SemaphoreType.DMA((len(operands),)),
        ],
        compiler_params=pltpu.CompilerParams(
            collective_id=0, has_side_effects=True, vmem_limit_bytes=60 * 1024 * 1024
        ),
    )(kriging.reshape(blocks, sites, cond), *operands)


def solution(mesh):
    return jax.shard_map(
        functools.partial(per_device, mesh.shape["wide"], mesh.shape["narrow"]),
        mesh=mesh,
        in_specs=(
            P("wide", "narrow", None, None),
            P("wide", "narrow", None),
            P("wide", "narrow", None),
            P("wide", "narrow", None, None),
            P("wide", "narrow", None, None),
            P("wide", "narrow", None),
            P("wide", "narrow", None),
            P("wide", None, None),
            P("wide", None),
            P("wide", None),
            P("wide", None, None),
            P(),
        ),
        out_specs=(P("wide", "narrow", None, None), P("wide", None, None)),
        check_vma=False,
    )
```

```python
import functools

import jax
import jax.numpy as jnp
from jax import lax
from jax.experimental import pallas as pl
from jax.experimental.pallas import tpu as pltpu
from jax.sharding import PartitionSpec as P

SHAPE_K = 1.25
EXACT = lax.Precision.HIGHEST
MESH = pl.DeviceIdType.MESH
NT = (((1,), (1,)), ((), ()))
NN = (((1,), (0,)), ((), ()))
TN = (((0,), (0,)), ((), ()))

RUN = 4
SLICES = 8
PARTS = 4

AROUND = [(dy, dz, dc) for dy in (0, 1, -1) for dz in (0, 1, -1) for dc in (0, 1)]


def taken(dy, dz):
    if dy and dz:
        return (0 if dy > 0 else 2) + (0 if dz > 0 else 1), 1
    if dy or dz:
        return (0 if dy + dz > 0 else 2), 2
    return 0, PARTS


STARTS = [sum(taken(-dy, -dz)[1] for dy, dz, _ in AROUND[:e]) for e in range(len(AROUND))]


def weibull(field, counts, offset):
    return SHAPE_K * (
        jnp.exp(SHAPE_K * (jnp.log(counts.astype(jnp.float32)) - offset - field)) - 1.0
    )


def two(x):
    high = x.astype(jnp.bfloat16)
    return high, (x - high.astype(jnp.float32)).astype(jnp.bfloat16)


def three(x):
    high = x.astype(jnp.bfloat16)
    rest = x - high.astype(jnp.float32)
    middle = rest.astype(jnp.bfloat16)
    return high, middle, (rest - middle.astype(jnp.float32)).astype(jnp.bfloat16)


def dot(a, b, dims):
    return lax.dot_general(a, b, dims, preferred_element_type=jnp.float32)


def dot_split(x, high, low, dims):
    rows = x.shape[0]
    x_high, x_low = two(x)
    both = dot(jnp.concatenate([x_high, x_low], axis=0), high, dims)
    return both[:rows] + both[rows:] + dot(x_high, low, dims)


def dot_pick(pick, values, dims):
    parts = [dot(pick, part, dims) for part in three(values)]
    return parts[0] + (parts[1] + parts[2])


def kernel(
    wide_count,
    narrow_count,
    kriging_ref,
    *refs,
):
    inputs, (fine_out, coarse_out), held_here = refs[:11], refs[11:13], refs[13:24]
    (
        field_ref,
        counts_ref,
        offset_ref,
        whiten_ref,
        near_ref,
        list_ref,
        home_ref,
        coarse_ref,
        coarse_counts_ref,
        coarse_offset_ref,
        coarse_whiten_ref,
    ) = held_here
    (
        weights,
        weights_high,
        weights_low,
        gain_high,
        gain_low,
        padded,
        rim,
        rim_in,
        own_slices,
        slices,
        picks,
        all_picks,
        far_send,
        far_recv,
        far,
        back_near,
        resid,
        back_white,
        terms_send,
        terms_recv,
        sums,
        sums_beside,
        plane_sums,
        sums_in,
        totals,
        spots,
        weight_sems,
        sems,
        copy_sems,
    ) = refs[24:]
    rows_here, cols_here, chains, sites = field_ref.shape
    blocks = rows_here * cols_here
    owned = coarse_ref.shape[0]
    near_count, far_count = near_ref.shape[2], list_ref.shape[0]
    reads = blocks * far_count
    coarse_total = owned * wide_count
    piece = chains // SLICES
    quarter = reads // PARTS
    tile = owned * piece
    message = reads * piece
    near_sites = near_count * sites

    w = lax.axis_index("wide")
    n = lax.axis_index("narrow")
    half = lax.rem(w // 8, 2)
    mine = lax.rem(n, 4) + 4 * half
    planes = wide_count // RUN
    x, plane = lax.rem(w, RUN), w // RUN
    place = x * planes + plane

    def sem(i):
        return sems.at[i]

    core, high = lax.rem(n, 2), lax.rem(plane, 2)
    depth = planes // 2
    y, z = high * 4 + n // 2, plane // 2
    members = []
    for dy, dz, dc in AROUND:
        to_y, to_z = lax.rem(y + dy + 8, 8), lax.rem(z + dz + depth, depth)
        to_core = 1 - core if dc else core
        members.append(
            (
                (to_z * 2 + to_y // 4) * RUN + x,
                lax.rem(to_y, 4) * 2 + to_core,
                to_core + 2 * lax.rem(to_y, 2) + 4 * lax.rem(to_z, 2),
            )
        )
    up, down = lax.rem(w + 1, wide_count), lax.rem(w + wide_count - 1, wide_count)
    right, left = lax.rem(n + 1, narrow_count), lax.rem(n + narrow_count - 1, narrow_count)

    barrier = pltpu.get_barrier_semaphore()

    def greet(to_w, to_n):
        pl.semaphore_signal(barrier, inc=1, device_id=(to_w, to_n), device_id_type=MESH)

    def across(t):
        return lax.rem(plane + t, planes)

    def beside(t):
        return lax.rem(x + t, RUN)

    def column(to):
        return lax.rem(n + (narrow_count // 2) * lax.rem(to + plane, 2), narrow_count)

    def greet_planes(t, carry):
        greet(across(t) * RUN + x, column(across(t)))
        return carry

    lax.fori_loop(1, planes, greet_planes, 0)
    for t in range(1, RUN):
        greet(plane * RUN + beside(t), n)
    for t in range(1, narrow_count):
        greet(w, lax.rem(n + t, narrow_count))
    for to_w, to_n, _ in members[1:]:
        greet(to_w, to_n)
    greet(up, n)
    greet(down, n)
    greetings = planes - 1 + RUN - 1 + narrow_count - 1 + len(AROUND) - 1 + 2

    copies = {}
    for i in (7, 4, 5, 6, 0, 1, 2, 8, 9, 10, 3):
        copies[i] = pltpu.make_async_copy(inputs[i], held_here[i], copy_sems.at[i])
        copies[i].start()
    weight_copies = [
        pltpu.make_async_copy(kriging_ref.at[b], weights.at[b], weight_sems.at[b])
        for b in range(blocks)
    ]
    for copy in weight_copies:
        copy.start()

    copies[7].wait()
    for s in range(SLICES):
        for j in range(owned):
            own_slices[s, j * piece : (j + 1) * piece, :] = coarse_ref[
                j, s * piece : (s + 1) * piece, :
            ]

    pl.semaphore_wait(barrier, greetings)
    own_rows = pl.ds(pl.multiple_of(place * tile, tile), tile)
    own_copy = pltpu.make_async_copy(own_slices.at[mine], slices.at[own_rows], sem(1))
    own_copy.start()

    def send_slice(t, carry):
        to = across(t) * RUN + x
        part = lax.rem(n, 4) + 4 * lax.rem(to // 8, 2)
        pltpu.make_async_remote_copy(
            src_ref=own_slices.at[part],
            dst_ref=slices.at[own_rows],
            send_sem=sem(0),
            recv_sem=sem(1),
            device_id=(to, column(across(t))),
            device_id_type=MESH,
        ).start()
        return carry

    lax.fori_loop(1, planes, send_slice, 0)

    copies[0].wait()

    def send(source, target, i, to_w, to_n):
        pltpu.make_async_remote_copy(
            src_ref=source,
            dst_ref=target,
            send_sem=sem(i),
            recv_sem=sem(i + 1),
            device_id=(to_w, to_n),
            device_id_type=MESH,
        ).start()

    def arrived(i, rows):
        part = padded.at[pl.ds(0, rows)]
        pltpu.make_async_copy(part, part, sem(i)).wait()

    rows_mid, cols_mid = pl.ds(1, rows_here), pl.ds(1, cols_here)
    far_r, far_c = rows_here + 1, cols_here + 1
    send(field_ref.at[rows_here - 1], padded.at[0, cols_mid], 4, up, n)
    send(field_ref.at[0], padded.at[far_r, cols_mid], 4, down, n)
    send(field_ref.at[:, cols_here - 1], padded.at[rows_mid, 0], 20, w, right)
    send(field_ref.at[:, 0], padded.at[rows_mid, far_c], 20, w, left)

    copies[5].wait()
    copies[6].wait()
    lane = lax.broadcasted_iota(jnp.int32, (1, coarse_total), 1)
    for i in range(blocks):
        for j in range(far_count):
            number = list_ref[j, i % cols_here, i // cols_here]
            owner, which = home_ref[number] // owned, lax.rem(home_ref[number], owned)
            at = (lax.rem(owner, RUN) * planes + owner // RUN) * owned + which
            q, i_q = divmod(i * far_count + j, quarter)
            picks[0, q, i_q : i_q + 1, :] = (lane == at).astype(jnp.float32)

    for (dy, dz, dc), (to_w, to_n, _) in zip(AROUND[1:], members[1:]):
        first, count = taken(dy, dz)
        send(
            picks.at[0, pl.ds(first, count)],
            picks.at[AROUND.index((-dy, -dz, dc)), pl.ds(first, count)],
            2,
            to_w,
            to_n,
        )
    for r in range(rows_here):
        for c in range(cols_here):
            padded[r + 1, c + 1] = field_ref[r, c]

    def run_rows(at):
        return pl.ds(pl.multiple_of(at * planes * tile, planes * tile), planes * tile)

    gathered_here = slices.at[run_rows(x)]
    pltpu.make_async_copy(gathered_here, gathered_here, sem(1)).wait()
    for t in range(1, RUN):
        pltpu.make_async_remote_copy(
            src_ref=gathered_here,
            dst_ref=gathered_here,
            send_sem=sem(16),
            recv_sem=sem(17),
            device_id=(plane * RUN + beside(t), n),
            device_id_type=MESH,
        ).start()
    other_runs = slices.at[pl.ds(0, (RUN - 1) * planes * tile)]

    copies[4].wait()
    for b in range(blocks):
        r, c = b // cols_here, b % cols_here
        for k in range(near_count):
            number = near_ref[r, c, k]
            grid_cols = cols_here * narrow_count
            row = number // grid_cols - w * rows_here + 1
            row = jnp.where(row < 0, row + rows_here * wide_count, row)
            row = jnp.where(row > rows_here + 1, row - rows_here * wide_count, row)
            col = lax.rem(number, grid_cols) - n * cols_here + 1
            col = jnp.where(col < 0, col + grid_cols, col)
            col = jnp.where(col > cols_here + 1, col - grid_cols, col)
            row, col = jnp.clip(row, 0, rows_here + 1), jnp.clip(col, 0, cols_here + 1)
            spots[b * near_count + k] = row * (cols_here + 2) + col

    for i in (1, 2, 3, 8, 9, 10):
        copies[i].wait()
    for b in range(blocks):
        gain = lax.dot_general(
            whiten_ref[b], whiten_ref[b], TN, precision=EXACT, preferred_element_type=jnp.float32
        )
        gain_high[b], gain_low[b] = two(gain)
    for j in range(owned):
        white = lax.dot_general(
            coarse_ref[j], coarse_whiten_ref[j], NT, precision=EXACT,
            preferred_element_type=jnp.float32,
        )
        prior = lax.dot_general(
            white, coarse_whiten_ref[j], NN, precision=EXACT, preferred_element_type=jnp.float32
        )
        coarse_out[j] = (
            weibull(coarse_ref[j], coarse_counts_ref[j : j + 1, :], coarse_offset_ref[j : j + 1, :])
            - prior
        )
    for b in range(blocks):
        r, c = b // cols_here, b % cols_here
        fine_out[r, c] = weibull(
            field_ref[r, c], counts_ref[b : b + 1, :], offset_ref[b : b + 1, :]
        )
        weight_copies[b].wait()
        weights_high[b], weights_low[b] = two(weights[b])
        back_near[b, near_count] = jnp.zeros((chains, sites), jnp.float32)

    arrived(5, 1)
    for e in (0, far_r):
        send(padded.at[e, cols_here], padded.at[e, 0], 22, w, right)
        send(padded.at[e, 1], padded.at[e, far_c], 22, w, left)

    pltpu.make_async_copy(other_runs, other_runs, sem(17)).wait()
    other_picks = picks.at[pl.ds(0, SLICES - 1)]
    pltpu.make_async_copy(other_picks, other_picks, sem(3)).wait()
    held = jnp.concatenate(
        [slices[pl.ds(r, coarse_total, stride=piece), :] for r in range(piece)], axis=1
    )
    for e, (dy, dz, _) in enumerate(AROUND):
        first, count = taken(-dy, -dz)
        for q in range(count):
            row = (STARTS[e] + q) * quarter
            all_picks[row : row + quarter, :] = picks[e, first + q, :quarter, :]
    pick = all_picks[...].astype(jnp.bfloat16)
    chosen = dot_pick(pick, held, NN)
    for r in range(piece):
        far_send[pl.ds(r, SLICES * reads, stride=piece), :] = chosen[:, r * sites : (r + 1) * sites]

    rows_part = quarter * piece

    def by_slice(ref, s, first, count):
        row = pl.multiple_of(s * message + first * rows_part, rows_part)
        return ref.at[pl.ds(row, count * rows_part)]

    def by_device(ref, e, count):
        return ref.at[pl.ds(STARTS[e] * rows_part, count * rows_part)]

    pltpu.make_async_copy(
        by_device(far_send, 0, PARTS), by_slice(far_recv, mine, 0, PARTS), sem(7)
    ).start()
    for e in range(1, len(AROUND)):
        (dy, dz, _), (to_w, to_n, _) = AROUND[e], members[e]
        first, count = taken(-dy, -dz)
        send(by_device(far_send, e, count), by_slice(far_recv, mine, first, count), 6, to_w, to_n)

    arrived(21, 2)
    arrived(23, 1)
    width = cols_here + 2
    for b in range(blocks):
        r, c = b // cols_here, b % cols_here
        fields = []
        for k in range(near_count):
            spot = spots[b * near_count + k]
            fields.append(padded[spot // width, lax.rem(spot, width)])
        near = jnp.concatenate(fields, axis=1)
        resid[b] = field_ref[r, c] - dot_split(
            near, weights_high[b, :, :near_sites], weights_low[b, :, :near_sites], NT
        )

    pltpu.make_async_copy(far_recv, far_recv, sem(7)).wait()
    for s in range(SLICES):
        for i in range(reads):
            far[i, s * piece : (s + 1) * piece, :] = far_recv[
                s * message + i * piece : s * message + (i + 1) * piece, :
            ]
    for b in range(blocks):
        distant = jnp.concatenate([far[b * far_count + j] for j in range(far_count)], axis=1)
        left_over = resid[b] - dot_split(
            distant, weights_high[b, :, near_sites:], weights_low[b, :, near_sites:], NT
        )
        back_white[b] = dot_split(left_over, gain_high[b], gain_low[b], NN)
    for b in range(blocks):
        back = dot_split(
            back_white[b], weights_high[b, :, near_sites:], weights_low[b, :, near_sites:], NN
        )
        for j in range(far_count):
            i = b * far_count + j
            for s in range(SLICES):
                terms_send[s * message + i * piece : s * message + (i + 1) * piece, :] = back[
                    s * piece : (s + 1) * piece, j * sites : (j + 1) * sites
                ]
    pltpu.make_async_copy(
        by_slice(terms_send, mine, 0, PARTS), by_device(terms_recv, 0, PARTS), sem(9)
    ).start()
    for (dy, dz, dc), (to_w, to_n, s) in zip(AROUND[1:], members[1:]):
        first, count = taken(dy, dz)
        there = AROUND.index((-dy, -dz, dc))
        send(
            by_slice(terms_send, s, first, count), by_device(terms_recv, there, count), 8, to_w, to_n
        )

    for b in range(blocks):
        back = dot_split(
            back_white[b], weights_high[b, :, :near_sites], weights_low[b, :, :near_sites], NN
        )
        for k in range(near_count):
            back_near[b, k] = back[:, k * sites : (k + 1) * sites]
    for pr in range(rows_here + 2):
        for pc in range(cols_here + 2):
            total = None
            for b in range(blocks):
                r, c = b // cols_here + 1, b % cols_here + 1
                if max(abs(r - pr), abs(c - pc)) != 1:
                    continue
                slot = jnp.int32(near_count)
                for k in range(near_count):
                    slot = jnp.where(
                        spots[b * near_count + k] == pr * width + pc, jnp.int32(k), slot
                    )
                term = back_near[b, slot]
                total = term if total is None else total + term
            rim[pr, pc] = total
    for e in (0, far_r):
        send(rim.at[e, far_c], rim_in.at[e, 0], 10, w, right)
        send(rim.at[e, 0], rim_in.at[e, far_c], 10, w, left)
    send(rim.at[rows_mid, far_c], rim_in.at[rows_mid, 0], 24, w, right)
    send(rim.at[rows_mid, 0], rim_in.at[rows_mid, far_c], 24, w, left)

    pltpu.make_async_copy(terms_recv, terms_recv, sem(9)).wait()
    gathered = jnp.concatenate(
        [terms_recv[pl.ds(r, SLICES * reads, stride=piece), :] for r in range(piece)], axis=1
    )
    summed = dot_pick(pick, gathered, TN)
    for r in range(piece):
        sums[pl.ds(r, coarse_total, stride=piece), :] = summed[:, r * sites : (r + 1) * sites]

    pltpu.make_async_copy(sums.at[run_rows(x)], sums_beside.at[x], sem(19)).start()
    for t in range(1, RUN):
        pltpu.make_async_remote_copy(
            src_ref=sums.at[run_rows(beside(t))],
            dst_ref=sums_beside.at[x],
            send_sem=sem(18),
            recv_sem=sem(19),
            device_id=(plane * RUN + beside(t), n),
            device_id_type=MESH,
        ).start()

    arrived(11, 1)
    for e in (0, far_r):
        rim[e, 1] = rim[e, 1] + rim_in[e, 0]
        rim[e, cols_here] = rim[e, cols_here] + rim_in[e, far_c]
    send(rim.at[far_r, cols_mid], rim_in.at[0, cols_mid], 26, up, n)
    send(rim.at[0, cols_mid], rim_in.at[far_r, cols_mid], 26, down, n)

    pltpu.make_async_copy(sums_beside, sums_beside, sem(19)).wait()
    plane_sums[...] = jnp.sum(sums_beside[...], axis=0).reshape(planes, tile, sites)
    pltpu.make_async_copy(plane_sums.at[plane], sums_in.at[plane], sem(13)).start()

    def send_sums(t, carry):
        pltpu.make_async_remote_copy(
            src_ref=plane_sums.at[across(t)],
            dst_ref=sums_in.at[plane],
            send_sem=sem(12),
            recv_sem=sem(13),
            device_id=(across(t) * RUN + x, column(across(t))),
            device_id_type=MESH,
        ).start()
        return carry

    lax.fori_loop(1, planes, send_sums, 0)

    arrived(25, 2)
    arrived(27, 1)
    for r in range(rows_here):
        for c in range(cols_here):
            total = fine_out[r, c] - back_white[r * cols_here + c] + rim[r + 1, c + 1]
            for e, at in ((0, 0), (far_r, rows_here - 1)):
                if r == at:
                    total = total + rim_in[e, c + 1]
            for e, at in ((0, 0), (far_c, cols_here - 1)):
                if c == at:
                    total = total + rim_in[r + 1, e]
            fine_out[r, c] = total

    pltpu.make_async_copy(sums_in, sums_in, sem(13)).wait()
    totals[n] = jnp.sum(
        sums_in[...].reshape(planes // 4, 2, 2, tile, sites), axis=(0, 2)
    )
    for t in range(1, narrow_count):
        pltpu.make_async_remote_copy(
            src_ref=totals.at[n],
            dst_ref=totals.at[n],
            send_sem=sem(14),
            recv_sem=sem(15),
            device_id=(w, lax.rem(n + t, narrow_count)),
            device_id_type=MESH,
        ).start()
    other_totals = totals.at[pl.ds(0, narrow_count - 1)]
    pltpu.make_async_copy(other_totals, other_totals, sem(15)).wait()
    for s in range(SLICES):
        for j in range(owned):
            rows = slice(s * piece, (s + 1) * piece)
            coarse_out[j, rows, :] = (
                coarse_out[j, rows, :]
                + totals[s % 4, s // 4, j * piece : (j + 1) * piece, :]
                + totals[s % 4 + 4, s // 4, j * piece : (j + 1) * piece, :]
            )

    sent = sums_in.at[pl.ds(0, planes - 1)]
    pltpu.make_async_copy(sent, sent, sem(0)).wait()
    pltpu.make_async_copy(other_runs, other_runs, sem(16)).wait()
    pltpu.make_async_copy(other_runs, other_runs, sem(18)).wait()
    pltpu.make_async_copy(other_picks, other_picks, sem(2)).wait()
    others = far_send.at[pl.ds(0, (SLICES - 1) * message)]
    pltpu.make_async_copy(others, others, sem(6)).wait()
    pltpu.make_async_copy(others, others, sem(8)).wait()
    for i, rows in ((4, 1), (20, 2), (22, 1), (10, 1), (24, 2), (26, 1)):
        arrived(i, rows)
    pltpu.make_async_copy(sent, sent, sem(12)).wait()

    pltpu.make_async_copy(other_totals, other_totals, sem(14)).wait()


def per_device(
    wide_count,
    narrow_count,
    fine_field,
    fine_counts,
    fine_offset,
    kriging,
    whiten,
    neighbours,
    coarse_list,
    coarse_field,
    coarse_counts,
    coarse_offset,
    coarse_whiten,
    coarse_home,
):
    rows_here, cols_here, chains, sites = fine_field.shape
    blocks = rows_here * cols_here
    owned = coarse_field.shape[0]
    cond = kriging.shape[3]
    near_count, far_count = neighbours.shape[2], coarse_list.shape[2]
    reads = blocks * far_count
    piece = chains // SLICES
    f32, bf16 = jnp.float32, jnp.bfloat16
    vmem = pl.BlockSpec(memory_space=pltpu.VMEM)
    operands = (
        fine_field,
        fine_counts.reshape(blocks, sites),
        fine_offset.reshape(blocks, sites),
        whiten.reshape(blocks, sites, sites),
        neighbours,
        coarse_list.transpose(2, 1, 0),
        coarse_home,
        coarse_field,
        coarse_counts,
        coarse_offset,
        coarse_whiten,
    )
    return pl.pallas_call(
        functools.partial(kernel, wide_count, narrow_count),
        out_shape=(
            pltpu.VMEM(fine_field.shape, f32),
            pltpu.VMEM(coarse_field.shape, f32),
        ),
        in_specs=[pl.BlockSpec(memory_space=pltpu.HBM)] * (1 + len(operands)),
        out_specs=(vmem, vmem),
        scratch_shapes=[
            (pltpu.SMEM if i in (4, 5, 6) else pltpu.VMEM)(x.shape, x.dtype)
            for i, x in enumerate(operands)
        ]
        + [
            pltpu.VMEM((blocks, sites, cond), f32),
            pltpu.VMEM((blocks, sites, cond), bf16),
            pltpu.VMEM((blocks, sites, cond), bf16),
            pltpu.VMEM((blocks, sites, sites), bf16),
            pltpu.VMEM((blocks, sites, sites), bf16),
            pltpu.VMEM((rows_here + 2, cols_here + 2, chains, sites), f32),
            pltpu.VMEM((rows_here + 2, cols_here + 2, chains, sites), f32),
            pltpu.VMEM((rows_here + 2, cols_here + 2, chains, sites), f32),
            pltpu.VMEM((SLICES, owned * piece, sites), f32),
            pltpu.VMEM((wide_count * owned * piece, sites), f32),
            pltpu.VMEM((len(AROUND), PARTS, 8, wide_count * owned), f32),
            pltpu.VMEM((reads * SLICES, wide_count * owned), f32),
            pltpu.VMEM((SLICES * reads * piece, sites), f32),
            pltpu.VMEM((SLICES * reads * piece, sites), f32),
            pltpu.VMEM((reads, chains, sites), f32),
            pltpu.VMEM((blocks, near_count + 1, chains, sites), f32),
            pltpu.VMEM((blocks, chains, sites), f32),
            pltpu.VMEM((blocks, chains, sites), f32),
            pltpu.VMEM((SLICES * reads * piece, sites), f32),
            pltpu.VMEM((SLICES * reads * piece, sites), f32),
            pltpu.VMEM((wide_count * owned * piece, sites), f32),
            pltpu.VMEM((RUN, wide_count // RUN * owned * piece, sites), f32),
            pltpu.VMEM((wide_count // RUN, owned * piece, sites), f32),
            pltpu.VMEM((wide_count // RUN, owned * piece, sites), f32),
            pltpu.VMEM((narrow_count, 2, owned * piece, sites), f32),
            pltpu.SMEM((blocks * near_count,), jnp.int32),
            pltpu.SemaphoreType.DMA((blocks,)),
            pltpu.SemaphoreType.DMA((28,)),
            pltpu.SemaphoreType.DMA((len(operands),)),
        ],
        compiler_params=pltpu.CompilerParams(
            collective_id=0, has_side_effects=True, vmem_limit_bytes=60 * 1024 * 1024
        ),
    )(kriging.reshape(blocks, sites, cond), *operands)


def solution(mesh):
    return jax.shard_map(
        functools.partial(per_device, mesh.shape["wide"], mesh.shape["narrow"]),
        mesh=mesh,
        in_specs=(
            P("wide", "narrow", None, None),
            P("wide", "narrow", None),
            P("wide", "narrow", None),
            P("wide", "narrow", None, None),
            P("wide", "narrow", None, None),
            P("wide", "narrow", None),
            P("wide", "narrow", None),
            P("wide", None, None),
            P("wide", None),
            P("wide", None),
            P("wide", None, None),
            P(),
        ),
        out_specs=(P("wide", "narrow", None, None), P("wide", None, None)),
        check_vma=False,
    )
```

```python
import functools

import jax
import jax.numpy as jnp
from jax import lax
from jax.experimental import pallas as pl
from jax.experimental.pallas import tpu as pltpu
from jax.sharding import PartitionSpec as P

SHAPE_K = 1.25
EXACT = lax.Precision.HIGHEST
MESH = pl.DeviceIdType.MESH
NT = (((1,), (1,)), ((), ()))
NN = (((1,), (0,)), ((), ()))
TN = (((0,), (0,)), ((), ()))

RUN = 4
SLICES = 8
PARTS = 4

AROUND = [(dy, dz, dc) for dy in (0, 1, -1) for dz in (0, 1, -1) for dc in (0, 1)]


def taken(dy, dz):
    if dy and dz:
        return (0 if dy > 0 else 2) + (0 if dz > 0 else 1), 1
    if dy or dz:
        return (0 if dy + dz > 0 else 2), 2
    return 0, PARTS


STARTS = [sum(taken(-dy, -dz)[1] for dy, dz, _ in AROUND[:e]) for e in range(len(AROUND))]


def weibull(field, counts, offset):
    return SHAPE_K * (
        jnp.exp(SHAPE_K * (jnp.log(counts.astype(jnp.float32)) - offset - field)) - 1.0
    )


def two(x):
    high = x.astype(jnp.bfloat16)
    return high, (x - high.astype(jnp.float32)).astype(jnp.bfloat16)


def three(x):
    high = x.astype(jnp.bfloat16)
    rest = x - high.astype(jnp.float32)
    middle = rest.astype(jnp.bfloat16)
    return high, middle, (rest - middle.astype(jnp.float32)).astype(jnp.bfloat16)


def dot(a, b, dims):
    return lax.dot_general(a, b, dims, preferred_element_type=jnp.float32)


def dot_split(x, high, low, dims):
    rows = x.shape[0]
    x_high, x_low = two(x)
    both = dot(jnp.concatenate([x_high, x_low], axis=0), high, dims)
    return both[:rows] + both[rows:] + dot(x_high, low, dims)


def dot_pick(pick, values, dims):
    parts = [dot(pick, part, dims) for part in three(values)]
    return parts[0] + (parts[1] + parts[2])


def kernel(
    wide_count,
    narrow_count,
    kriging_ref,
    *refs,
):
    inputs, (fine_out, coarse_out), held_here = refs[:11], refs[11:13], refs[13:24]
    (
        field_ref,
        counts_ref,
        offset_ref,
        whiten_ref,
        near_ref,
        list_ref,
        home_ref,
        coarse_ref,
        coarse_counts_ref,
        coarse_offset_ref,
        coarse_whiten_ref,
    ) = held_here
    (
        weights,
        weights_high,
        weights_low,
        gain_high,
        gain_low,
        gains,
        reach_high,
        reach_low,
        padded,
        rim,
        rim_in,
        own_slices,
        slices,
        picks,
        all_picks,
        far_send,
        far_recv,
        far,
        back_near,
        resid,
        back_white,
        terms_send,
        terms_recv,
        sums,
        sums_beside,
        plane_sums,
        sums_in,
        totals,
        spots,
        weight_sems,
        sems,
        copy_sems,
    ) = refs[24:]
    rows_here, cols_here, chains, sites = field_ref.shape
    blocks = rows_here * cols_here
    owned = coarse_ref.shape[0]
    near_count, far_count = near_ref.shape[2], list_ref.shape[0]
    reads = blocks * far_count
    coarse_total = owned * wide_count
    piece = chains // SLICES
    quarter = reads // PARTS
    tile = owned * piece
    message = reads * piece
    near_sites = near_count * sites

    w = lax.axis_index("wide")
    n = lax.axis_index("narrow")
    half = lax.rem(w // 8, 2)
    mine = lax.rem(n, 4) + 4 * half
    planes = wide_count // RUN
    x, plane = lax.rem(w, RUN), w // RUN
    place = x * planes + plane

    def sem(i):
        return sems.at[i]

    core, high = lax.rem(n, 2), lax.rem(plane, 2)
    depth = planes // 2
    y, z = high * 4 + n // 2, plane // 2
    members = []
    for dy, dz, dc in AROUND:
        to_y, to_z = lax.rem(y + dy + 8, 8), lax.rem(z + dz + depth, depth)
        to_core = 1 - core if dc else core
        members.append(
            (
                (to_z * 2 + to_y // 4) * RUN + x,
                lax.rem(to_y, 4) * 2 + to_core,
                to_core + 2 * lax.rem(to_y, 2) + 4 * lax.rem(to_z, 2),
            )
        )
    up, down = lax.rem(w + 1, wide_count), lax.rem(w + wide_count - 1, wide_count)
    right, left = lax.rem(n + 1, narrow_count), lax.rem(n + narrow_count - 1, narrow_count)

    copies = {
        i: pltpu.make_async_copy(inputs[i], held_here[i], copy_sems.at[i])
        for i in range(len(inputs))
    }
    copies[7].start()

    barrier = pltpu.get_barrier_semaphore()

    def greet(to_w, to_n):
        pl.semaphore_signal(barrier, inc=1, device_id=(to_w, to_n), device_id_type=MESH)

    def across(t):
        return lax.rem(plane + t, planes)

    def beside(t):
        return lax.rem(x + t, RUN)

    def column(to):
        return lax.rem(n + (narrow_count // 2) * lax.rem(to + plane, 2), narrow_count)

    def greet_planes(t, carry):
        greet(across(t) * RUN + x, column(across(t)))
        return carry

    lax.fori_loop(1, planes, greet_planes, 0)
    for t in range(1, RUN):
        greet(plane * RUN + beside(t), n)
    for t in range(1, narrow_count):
        greet(w, lax.rem(n + t, narrow_count))
    for to_w, to_n, _ in members[1:]:
        greet(to_w, to_n)
    greet(up, n)
    greet(down, n)
    greetings = planes - 1 + RUN - 1 + narrow_count - 1 + len(AROUND) - 1 + 2

    for i in (0, 4, 5, 6, 1, 2, 8, 9, 10, 3):
        copies[i].start()
    weight_copies = [
        pltpu.make_async_copy(kriging_ref.at[b], weights.at[b], weight_sems.at[b])
        for b in range(blocks)
    ]
    for copy in weight_copies:
        copy.start()

    copies[7].wait()
    for s in range(SLICES):
        for j in range(owned):
            own_slices[s, j * piece : (j + 1) * piece, :] = coarse_ref[
                j, s * piece : (s + 1) * piece, :
            ]

    pl.semaphore_wait(barrier, greetings)
    own_rows = pl.ds(pl.multiple_of(place * tile, tile), tile)
    own_copy = pltpu.make_async_copy(own_slices.at[mine], slices.at[own_rows], sem(1))
    own_copy.start()

    def send_slice(t, carry):
        to = across(t) * RUN + x
        part = lax.rem(n, 4) + 4 * lax.rem(to // 8, 2)
        pltpu.make_async_remote_copy(
            src_ref=own_slices.at[part],
            dst_ref=slices.at[own_rows],
            send_sem=sem(0),
            recv_sem=sem(1),
            device_id=(to, column(across(t))),
            device_id_type=MESH,
        ).start()
        return carry

    lax.fori_loop(1, planes, send_slice, 0)

    copies[0].wait()

    def send(source, target, i, to_w, to_n):
        pltpu.make_async_remote_copy(
            src_ref=source,
            dst_ref=target,
            send_sem=sem(i),
            recv_sem=sem(i + 1),
            device_id=(to_w, to_n),
            device_id_type=MESH,
        ).start()

    def arrived(i, rows):
        part = padded.at[pl.ds(0, rows)]
        pltpu.make_async_copy(part, part, sem(i)).wait()

    rows_mid, cols_mid = pl.ds(1, rows_here), pl.ds(1, cols_here)
    far_r, far_c = rows_here + 1, cols_here + 1
    send(field_ref.at[rows_here - 1], padded.at[0, cols_mid], 4, up, n)
    send(field_ref.at[0], padded.at[far_r, cols_mid], 4, down, n)
    send(field_ref.at[:, cols_here - 1], padded.at[rows_mid, 0], 20, w, right)
    send(field_ref.at[:, 0], padded.at[rows_mid, far_c], 20, w, left)

    copies[5].wait()
    copies[6].wait()
    lane = lax.broadcasted_iota(jnp.int32, (1, coarse_total), 1)
    for i in range(blocks):
        for j in range(far_count):
            number = list_ref[j, i % cols_here, i // cols_here]
            owner, which = home_ref[number] // owned, lax.rem(home_ref[number], owned)
            at = (lax.rem(owner, RUN) * planes + owner // RUN) * owned + which
            q, i_q = divmod(i * far_count + j, quarter)
            picks[0, q, i_q : i_q + 1, :] = (lane == at).astype(jnp.float32)

    for (dy, dz, dc), (to_w, to_n, _) in zip(AROUND[1:], members[1:]):
        first, count = taken(dy, dz)
        send(
            picks.at[0, pl.ds(first, count)],
            picks.at[AROUND.index((-dy, -dz, dc)), pl.ds(first, count)],
            2,
            to_w,
            to_n,
        )
    for r in range(rows_here):
        for c in range(cols_here):
            padded[r + 1, c + 1] = field_ref[r, c]

    def run_rows(at):
        return pl.ds(pl.multiple_of(at * planes * tile, planes * tile), planes * tile)

    gathered_here = slices.at[run_rows(x)]
    pltpu.make_async_copy(gathered_here, gathered_here, sem(1)).wait()
    for t in range(1, RUN):
        pltpu.make_async_remote_copy(
            src_ref=gathered_here,
            dst_ref=gathered_here,
            send_sem=sem(16),
            recv_sem=sem(17),
            device_id=(plane * RUN + beside(t), n),
            device_id_type=MESH,
        ).start()
    other_runs = slices.at[pl.ds(0, (RUN - 1) * planes * tile)]

    copies[4].wait()
    for b in range(blocks):
        r, c = b // cols_here, b % cols_here
        for k in range(near_count):
            number = near_ref[r, c, k]
            grid_cols = cols_here * narrow_count
            row = number // grid_cols - w * rows_here + 1
            row = jnp.where(row < 0, row + rows_here * wide_count, row)
            row = jnp.where(row > rows_here + 1, row - rows_here * wide_count, row)
            col = lax.rem(number, grid_cols) - n * cols_here + 1
            col = jnp.where(col < 0, col + grid_cols, col)
            col = jnp.where(col > cols_here + 1, col - grid_cols, col)
            row, col = jnp.clip(row, 0, rows_here + 1), jnp.clip(col, 0, cols_here + 1)
            spots[b * near_count + k] = row * (cols_here + 2) + col

    for i in (1, 2, 3, 8, 9, 10):
        copies[i].wait()
    for b in range(blocks):
        gain = lax.dot_general(
            whiten_ref[b], whiten_ref[b], TN, precision=EXACT, preferred_element_type=jnp.float32
        )
        gains[b] = gain
        gain_high[b], gain_low[b] = two(gain)
    for j in range(owned):
        white = lax.dot_general(
            coarse_ref[j], coarse_whiten_ref[j], NT, precision=EXACT,
            preferred_element_type=jnp.float32,
        )
        prior = lax.dot_general(
            white, coarse_whiten_ref[j], NN, precision=EXACT, preferred_element_type=jnp.float32
        )
        coarse_out[j] = (
            weibull(coarse_ref[j], coarse_counts_ref[j : j + 1, :], coarse_offset_ref[j : j + 1, :])
            - prior
        )
    for b in range(blocks):
        r, c = b // cols_here, b % cols_here
        fine_out[r, c] = weibull(
            field_ref[r, c], counts_ref[b : b + 1, :], offset_ref[b : b + 1, :]
        )
        weight_copies[b].wait()
        weights_high[b], weights_low[b] = two(weights[b])
        reach = dot_split(gains[b], weights_high[b, :, near_sites:], weights_low[b, :, near_sites:], NN)
        reach_high[b], reach_low[b] = two(reach)
        back_near[b, near_count] = jnp.zeros((chains, sites), jnp.float32)

    arrived(5, 1)
    for e in (0, far_r):
        send(padded.at[e, cols_here], padded.at[e, 0], 22, w, right)
        send(padded.at[e, 1], padded.at[e, far_c], 22, w, left)

    pltpu.make_async_copy(other_runs, other_runs, sem(17)).wait()
    other_picks = picks.at[pl.ds(0, SLICES - 1)]
    pltpu.make_async_copy(other_picks, other_picks, sem(3)).wait()
    held = jnp.concatenate(
        [slices[pl.ds(r, coarse_total, stride=piece), :] for r in range(piece)], axis=1
    )
    for e, (dy, dz, _) in enumerate(AROUND):
        first, count = taken(-dy, -dz)
        for q in range(count):
            row = (STARTS[e] + q) * quarter
            all_picks[row : row + quarter, :] = picks[e, first + q, :quarter, :]
    pick = all_picks[...].astype(jnp.bfloat16)
    chosen = dot_pick(pick, held, NN)
    for r in range(piece):
        far_send[pl.ds(r, SLICES * reads, stride=piece), :] = chosen[:, r * sites : (r + 1) * sites]

    rows_part = quarter * piece

    def by_slice(ref, s, first, count):
        row = pl.multiple_of(s * message + first * rows_part, rows_part)
        return ref.at[pl.ds(row, count * rows_part)]

    def by_device(ref, e, count):
        return ref.at[pl.ds(STARTS[e] * rows_part, count * rows_part)]

    pltpu.make_async_copy(
        by_device(far_send, 0, PARTS), by_slice(far_recv, mine, 0, PARTS), sem(7)
    ).start()
    for e in range(1, len(AROUND)):
        (dy, dz, _), (to_w, to_n, _) = AROUND[e], members[e]
        first, count = taken(-dy, -dz)
        send(by_device(far_send, e, count), by_slice(far_recv, mine, first, count), 6, to_w, to_n)

    arrived(21, 2)
    arrived(23, 1)
    width = cols_here + 2
    for b in range(blocks):
        r, c = b // cols_here, b % cols_here
        fields = []
        for k in range(near_count):
            spot = spots[b * near_count + k]
            fields.append(padded[spot // width, lax.rem(spot, width)])
        near = jnp.concatenate(fields, axis=1)
        resid[b] = field_ref[r, c] - dot_split(
            near, weights_high[b, :, :near_sites], weights_low[b, :, :near_sites], NT
        )

    pltpu.make_async_copy(far_recv, far_recv, sem(7)).wait()
    for s in range(SLICES):
        for i in range(reads):
            far[i, s * piece : (s + 1) * piece, :] = far_recv[
                s * message + i * piece : s * message + (i + 1) * piece, :
            ]
    for b in range(blocks):
        distant = jnp.concatenate([far[b * far_count + j] for j in range(far_count)], axis=1)
        resid[b] = resid[b] - dot_split(
            distant, weights_high[b, :, near_sites:], weights_low[b, :, near_sites:], NT
        )
    for b in range(blocks):
        back = dot_split(resid[b], reach_high[b], reach_low[b], NN)
        for j in range(far_count):
            i = b * far_count + j
            for s in range(SLICES):
                terms_send[s * message + i * piece : s * message + (i + 1) * piece, :] = back[
                    s * piece : (s + 1) * piece, j * sites : (j + 1) * sites
                ]
    pltpu.make_async_copy(
        by_slice(terms_send, mine, 0, PARTS), by_device(terms_recv, 0, PARTS), sem(9)
    ).start()
    for (dy, dz, dc), (to_w, to_n, s) in zip(AROUND[1:], members[1:]):
        first, count = taken(dy, dz)
        there = AROUND.index((-dy, -dz, dc))
        send(
            by_slice(terms_send, s, first, count), by_device(terms_recv, there, count), 8, to_w, to_n
        )

    for b in range(blocks):
        back_white[b] = dot_split(resid[b], gain_high[b], gain_low[b], NN)
    for b in range(blocks):
        back = dot_split(
            back_white[b], weights_high[b, :, :near_sites], weights_low[b, :, :near_sites], NN
        )
        for k in range(near_count):
            back_near[b, k] = back[:, k * sites : (k + 1) * sites]
    for pr in range(rows_here + 2):
        for pc in range(cols_here + 2):
            total = None
            for b in range(blocks):
                r, c = b // cols_here + 1, b % cols_here + 1
                if max(abs(r - pr), abs(c - pc)) != 1:
                    continue
                slot = jnp.int32(near_count)
                for k in range(near_count):
                    slot = jnp.where(
                        spots[b * near_count + k] == pr * width + pc, jnp.int32(k), slot
                    )
                term = back_near[b, slot]
                total = term if total is None else total + term
            rim[pr, pc] = total
    for e in (0, far_r):
        send(rim.at[e, far_c], rim_in.at[e, 0], 10, w, right)
        send(rim.at[e, 0], rim_in.at[e, far_c], 10, w, left)
    send(rim.at[rows_mid, far_c], rim_in.at[rows_mid, 0], 24, w, right)
    send(rim.at[rows_mid, 0], rim_in.at[rows_mid, far_c], 24, w, left)

    pltpu.make_async_copy(terms_recv, terms_recv, sem(9)).wait()
    gathered = jnp.concatenate(
        [terms_recv[pl.ds(r, SLICES * reads, stride=piece), :] for r in range(piece)], axis=1
    )
    summed = dot_pick(pick, gathered, TN)
    for r in range(piece):
        sums[pl.ds(r, coarse_total, stride=piece), :] = summed[:, r * sites : (r + 1) * sites]

    pltpu.make_async_copy(sums.at[run_rows(x)], sums_beside.at[x], sem(19)).start()
    for t in range(1, RUN):
        pltpu.make_async_remote_copy(
            src_ref=sums.at[run_rows(beside(t))],
            dst_ref=sums_beside.at[x],
            send_sem=sem(18),
            recv_sem=sem(19),
            device_id=(plane * RUN + beside(t), n),
            device_id_type=MESH,
        ).start()

    arrived(11, 1)
    for e in (0, far_r):
        rim[e, 1] = rim[e, 1] + rim_in[e, 0]
        rim[e, cols_here] = rim[e, cols_here] + rim_in[e, far_c]
    send(rim.at[far_r, cols_mid], rim_in.at[0, cols_mid], 26, up, n)
    send(rim.at[0, cols_mid], rim_in.at[far_r, cols_mid], 26, down, n)

    pltpu.make_async_copy(sums_beside, sums_beside, sem(19)).wait()
    plane_sums[...] = jnp.sum(sums_beside[...], axis=0).reshape(planes, tile, sites)
    pltpu.make_async_copy(plane_sums.at[plane], sums_in.at[plane], sem(13)).start()

    def send_sums(t, carry):
        pltpu.make_async_remote_copy(
            src_ref=plane_sums.at[across(t)],
            dst_ref=sums_in.at[plane],
            send_sem=sem(12),
            recv_sem=sem(13),
            device_id=(across(t) * RUN + x, column(across(t))),
            device_id_type=MESH,
        ).start()
        return carry

    lax.fori_loop(1, planes, send_sums, 0)

    arrived(25, 2)
    arrived(27, 1)
    for r in range(rows_here):
        for c in range(cols_here):
            total = fine_out[r, c] - back_white[r * cols_here + c] + rim[r + 1, c + 1]
            for e, at in ((0, 0), (far_r, rows_here - 1)):
                if r == at:
                    total = total + rim_in[e, c + 1]
            for e, at in ((0, 0), (far_c, cols_here - 1)):
                if c == at:
                    total = total + rim_in[r + 1, e]
            fine_out[r, c] = total

    pltpu.make_async_copy(sums_in, sums_in, sem(13)).wait()
    totals[n] = jnp.sum(
        sums_in[...].reshape(planes // 4, 2, 2, tile, sites), axis=(0, 2)
    )
    for t in range(1, narrow_count):
        pltpu.make_async_remote_copy(
            src_ref=totals.at[n],
            dst_ref=totals.at[n],
            send_sem=sem(14),
            recv_sem=sem(15),
            device_id=(w, lax.rem(n + t, narrow_count)),
            device_id_type=MESH,
        ).start()
    other_totals = totals.at[pl.ds(0, narrow_count - 1)]
    pltpu.make_async_copy(other_totals, other_totals, sem(15)).wait()
    for s in range(SLICES):
        for j in range(owned):
            rows = slice(s * piece, (s + 1) * piece)
            coarse_out[j, rows, :] = (
                coarse_out[j, rows, :]
                + totals[s % 4, s // 4, j * piece : (j + 1) * piece, :]
                + totals[s % 4 + 4, s // 4, j * piece : (j + 1) * piece, :]
            )

    sent = sums_in.at[pl.ds(0, planes - 1)]
    pltpu.make_async_copy(sent, sent, sem(0)).wait()
    pltpu.make_async_copy(other_runs, other_runs, sem(16)).wait()
    pltpu.make_async_copy(other_runs, other_runs, sem(18)).wait()
    pltpu.make_async_copy(other_picks, other_picks, sem(2)).wait()
    others = far_send.at[pl.ds(0, (SLICES - 1) * message)]
    pltpu.make_async_copy(others, others, sem(6)).wait()
    pltpu.make_async_copy(others, others, sem(8)).wait()
    for i, rows in ((4, 1), (20, 2), (22, 1), (10, 1), (24, 2), (26, 1)):
        arrived(i, rows)
    pltpu.make_async_copy(sent, sent, sem(12)).wait()

    pltpu.make_async_copy(other_totals, other_totals, sem(14)).wait()


def per_device(
    wide_count,
    narrow_count,
    fine_field,
    fine_counts,
    fine_offset,
    kriging,
    whiten,
    neighbours,
    coarse_list,
    coarse_field,
    coarse_counts,
    coarse_offset,
    coarse_whiten,
    coarse_home,
):
    rows_here, cols_here, chains, sites = fine_field.shape
    blocks = rows_here * cols_here
    owned = coarse_field.shape[0]
    cond = kriging.shape[3]
    near_count, far_count = neighbours.shape[2], coarse_list.shape[2]
    reads = blocks * far_count
    piece = chains // SLICES
    f32, bf16 = jnp.float32, jnp.bfloat16
    vmem = pl.BlockSpec(memory_space=pltpu.VMEM)
    operands = (
        fine_field,
        fine_counts.reshape(blocks, sites),
        fine_offset.reshape(blocks, sites),
        whiten.reshape(blocks, sites, sites),
        neighbours,
        coarse_list.transpose(2, 1, 0),
        coarse_home,
        coarse_field,
        coarse_counts,
        coarse_offset,
        coarse_whiten,
    )
    return pl.pallas_call(
        functools.partial(kernel, wide_count, narrow_count),
        out_shape=(
            pltpu.VMEM(fine_field.shape, f32),
            pltpu.VMEM(coarse_field.shape, f32),
        ),
        in_specs=[pl.BlockSpec(memory_space=pltpu.HBM)] * (1 + len(operands)),
        out_specs=(vmem, vmem),
        scratch_shapes=[
            (pltpu.SMEM if i in (4, 5, 6) else pltpu.VMEM)(x.shape, x.dtype)
            for i, x in enumerate(operands)
        ]
        + [
            pltpu.VMEM((blocks, sites, cond), f32),
            pltpu.VMEM((blocks, sites, cond), bf16),
            pltpu.VMEM((blocks, sites, cond), bf16),
            pltpu.VMEM((blocks, sites, sites), bf16),
            pltpu.VMEM((blocks, sites, sites), bf16),
            pltpu.VMEM((blocks, sites, sites), f32),
            pltpu.VMEM((blocks, sites, far_count * sites), bf16),
            pltpu.VMEM((blocks, sites, far_count * sites), bf16),
            pltpu.VMEM((rows_here + 2, cols_here + 2, chains, sites), f32),
            pltpu.VMEM((rows_here + 2, cols_here + 2, chains, sites), f32),
            pltpu.VMEM((rows_here + 2, cols_here + 2, chains, sites), f32),
            pltpu.VMEM((SLICES, owned * piece, sites), f32),
            pltpu.VMEM((wide_count * owned * piece, sites), f32),
            pltpu.VMEM((len(AROUND), PARTS, 8, wide_count * owned), f32),
            pltpu.VMEM((reads * SLICES, wide_count * owned), f32),
            pltpu.VMEM((SLICES * reads * piece, sites), f32),
            pltpu.VMEM((SLICES * reads * piece, sites), f32),
            pltpu.VMEM((reads, chains, sites), f32),
            pltpu.VMEM((blocks, near_count + 1, chains, sites), f32),
            pltpu.VMEM((blocks, chains, sites), f32),
            pltpu.VMEM((blocks, chains, sites), f32),
            pltpu.VMEM((SLICES * reads * piece, sites), f32),
            pltpu.VMEM((SLICES * reads * piece, sites), f32),
            pltpu.VMEM((wide_count * owned * piece, sites), f32),
            pltpu.VMEM((RUN, wide_count // RUN * owned * piece, sites), f32),
            pltpu.VMEM((wide_count // RUN, owned * piece, sites), f32),
            pltpu.VMEM((wide_count // RUN, owned * piece, sites), f32),
            pltpu.VMEM((narrow_count, 2, owned * piece, sites), f32),
            pltpu.SMEM((blocks * near_count,), jnp.int32),
            pltpu.SemaphoreType.DMA((blocks,)),
            pltpu.SemaphoreType.DMA((28,)),
            pltpu.SemaphoreType.DMA((len(operands),)),
        ],
        compiler_params=pltpu.CompilerParams(
            collective_id=0, has_side_effects=True, vmem_limit_bytes=60 * 1024 * 1024
        ),
    )(kriging.reshape(blocks, sites, cond), *operands)


def solution(mesh):
    return jax.shard_map(
        functools.partial(per_device, mesh.shape["wide"], mesh.shape["narrow"]),
        mesh=mesh,
        in_specs=(
            P("wide", "narrow", None, None),
            P("wide", "narrow", None),
            P("wide", "narrow", None),
            P("wide", "narrow", None, None),
            P("wide", "narrow", None, None),
            P("wide", "narrow", None),
            P("wide", "narrow", None),
            P("wide", None, None),
            P("wide", None),
            P("wide", None),
            P("wide", None, None),
            P(),
        ),
        out_specs=(P("wide", "narrow", None, None), P("wide", None, None)),
        check_vma=False,
    )
```

```python
import functools

import jax
import jax.numpy as jnp
from jax import lax
from jax.experimental import pallas as pl
from jax.experimental.pallas import tpu as pltpu
from jax.sharding import PartitionSpec as P

SHAPE_K = 1.25
EXACT = lax.Precision.HIGHEST
MESH = pl.DeviceIdType.MESH
NT = (((1,), (1,)), ((), ()))
NN = (((1,), (0,)), ((), ()))
TN = (((0,), (0,)), ((), ()))

RUN = 4
SLICES = 8
PARTS = 4

AROUND = [(dy, dz, dc) for dy in (0, 1, -1) for dz in (0, 1, -1) for dc in (0, 1)]


def taken(dy, dz):
    if dy and dz:
        return (0 if dy > 0 else 2) + (0 if dz > 0 else 1), 1
    if dy or dz:
        return (0 if dy + dz > 0 else 2), 2
    return 0, PARTS


STARTS = [sum(taken(-dy, -dz)[1] for dy, dz, _ in AROUND[:e]) for e in range(len(AROUND))]


def weibull(field, counts, offset):
    return SHAPE_K * (
        jnp.exp(SHAPE_K * (jnp.log(counts.astype(jnp.float32)) - offset - field)) - 1.0
    )


def two(x):
    high = x.astype(jnp.bfloat16)
    return high, (x - high.astype(jnp.float32)).astype(jnp.bfloat16)


def three(x):
    high = x.astype(jnp.bfloat16)
    rest = x - high.astype(jnp.float32)
    middle = rest.astype(jnp.bfloat16)
    return high, middle, (rest - middle.astype(jnp.float32)).astype(jnp.bfloat16)


def dot(a, b, dims):
    return lax.dot_general(a, b, dims, preferred_element_type=jnp.float32)


def dot_split(x, high, low, dims):
    rows = x.shape[0]
    x_high, x_low = two(x)
    both = dot(jnp.concatenate([x_high, x_low], axis=0), high, dims)
    return both[:rows] + both[rows:] + dot(x_high, low, dims)


def dot_pick(pick, values, dims):
    parts = [dot(pick, part, dims) for part in three(values)]
    return parts[0] + (parts[1] + parts[2])


def kernel(
    wide_count,
    narrow_count,
    kriging_ref,
    *refs,
):
    inputs, (fine_out, coarse_out), held_here = refs[:11], refs[11:13], refs[13:24]
    (
        field_ref,
        counts_ref,
        offset_ref,
        whiten_ref,
        near_ref,
        list_ref,
        home_ref,
        coarse_ref,
        coarse_counts_ref,
        coarse_offset_ref,
        coarse_whiten_ref,
    ) = held_here
    (
        weights,
        weights_high,
        weights_low,
        gain_high,
        gain_low,
        gains,
        reach_high,
        reach_low,
        padded,
        rim,
        rim_in,
        own_slices,
        slices,
        picks,
        all_picks,
        far_send,
        far_recv,
        far,
        back_near,
        resid,
        back_white,
        terms_send,
        terms_recv,
        sums,
        sums_beside,
        plane_sums,
        sums_in,
        totals,
        spots,
        weight_sems,
        sems,
        copy_sems,
    ) = refs[24:]
    rows_here, cols_here, chains, sites = field_ref.shape
    blocks = rows_here * cols_here
    owned = coarse_ref.shape[0]
    near_count, far_count = near_ref.shape[2], list_ref.shape[0]
    reads = blocks * far_count
    coarse_total = owned * wide_count
    piece = chains // SLICES
    quarter = reads // PARTS
    tile = owned * piece
    message = reads * piece
    near_sites = near_count * sites

    w = lax.axis_index("wide")
    n = lax.axis_index("narrow")
    half = lax.rem(w // 8, 2)
    mine = lax.rem(n, 4) + 4 * half
    planes = wide_count // RUN
    x, plane = lax.rem(w, RUN), w // RUN
    place = x * planes + plane

    def sem(i):
        return sems.at[i]

    core, high = lax.rem(n, 2), lax.rem(plane, 2)
    depth = planes // 2
    y, z = high * 4 + n // 2, plane // 2
    members = []
    for dy, dz, dc in AROUND:
        to_y, to_z = lax.rem(y + dy + 8, 8), lax.rem(z + dz + depth, depth)
        to_core = 1 - core if dc else core
        members.append(
            (
                (to_z * 2 + to_y // 4) * RUN + x,
                lax.rem(to_y, 4) * 2 + to_core,
                to_core + 2 * lax.rem(to_y, 2) + 4 * lax.rem(to_z, 2),
            )
        )
    up, down = lax.rem(w + 1, wide_count), lax.rem(w + wide_count - 1, wide_count)
    right, left = lax.rem(n + 1, narrow_count), lax.rem(n + narrow_count - 1, narrow_count)

    copies = {
        i: pltpu.make_async_copy(inputs[i], held_here[i], copy_sems.at[i])
        for i in range(len(inputs))
    }
    copies[7].start()

    barrier = pltpu.get_barrier_semaphore()

    def greet(to_w, to_n):
        pl.semaphore_signal(barrier, inc=1, device_id=(to_w, to_n), device_id_type=MESH)

    def across(t):
        return lax.rem(plane + 1 + lax.rem(t + planes // 2 - 2, planes - 1), planes)

    def beside(t):
        return lax.rem(x + t, RUN)

    def column(to):
        return lax.rem(n + (narrow_count // 2) * lax.rem(to + plane, 2), narrow_count)

    def greet_planes(t, carry):
        greet(across(t) * RUN + x, column(across(t)))
        return carry

    lax.fori_loop(1, planes, greet_planes, 0)
    for t in (2, 1, 3):
        greet(plane * RUN + beside(t), n)
    for t in range(1, narrow_count):
        greet(w, lax.rem(n + t, narrow_count))
    for to_w, to_n, _ in members[1:]:
        greet(to_w, to_n)
    greet(up, n)
    greet(down, n)
    greetings = planes - 1 + RUN - 1 + narrow_count - 1 + len(AROUND) - 1 + 2

    for i in (0, 4, 5, 6, 1, 2, 8, 9, 10, 3):
        copies[i].start()
    weight_copies = [
        pltpu.make_async_copy(kriging_ref.at[b], weights.at[b], weight_sems.at[b])
        for b in range(blocks)
    ]
    for copy in weight_copies:
        copy.start()

    copies[7].wait()
    for s in range(SLICES):
        for j in range(owned):
            own_slices[s, j * piece : (j + 1) * piece, :] = coarse_ref[
                j, s * piece : (s + 1) * piece, :
            ]

    pl.semaphore_wait(barrier, greetings)
    own_rows = pl.ds(pl.multiple_of(place * tile, tile), tile)
    own_copy = pltpu.make_async_copy(own_slices.at[mine], slices.at[own_rows], sem(1))
    own_copy.start()

    def send_slice(t, carry):
        to = across(t) * RUN + x
        part = lax.rem(n, 4) + 4 * lax.rem(to // 8, 2)
        pltpu.make_async_remote_copy(
            src_ref=own_slices.at[part],
            dst_ref=slices.at[own_rows],
            send_sem=sem(0),
            recv_sem=sem(1),
            device_id=(to, column(across(t))),
            device_id_type=MESH,
        ).start()
        return carry

    lax.fori_loop(1, planes, send_slice, 0)

    copies[0].wait()

    def send(source, target, i, to_w, to_n):
        pltpu.make_async_remote_copy(
            src_ref=source,
            dst_ref=target,
            send_sem=sem(i),
            recv_sem=sem(i + 1),
            device_id=(to_w, to_n),
            device_id_type=MESH,
        ).start()

    def arrived(i, rows):
        part = padded.at[pl.ds(0, rows)]
        pltpu.make_async_copy(part, part, sem(i)).wait()

    rows_mid, cols_mid = pl.ds(1, rows_here), pl.ds(1, cols_here)
    far_r, far_c = rows_here + 1, cols_here + 1
    send(field_ref.at[rows_here - 1], padded.at[0, cols_mid], 4, up, n)
    send(field_ref.at[0], padded.at[far_r, cols_mid], 4, down, n)
    send(field_ref.at[:, cols_here - 1], padded.at[rows_mid, 0], 20, w, right)
    send(field_ref.at[:, 0], padded.at[rows_mid, far_c], 20, w, left)

    copies[5].wait()
    copies[6].wait()
    lane = lax.broadcasted_iota(jnp.int32, (1, coarse_total), 1)
    for i in range(blocks):
        for j in range(far_count):
            number = list_ref[j, i % cols_here, i // cols_here]
            owner, which = home_ref[number] // owned, lax.rem(home_ref[number], owned)
            at = (lax.rem(owner, RUN) * planes + owner // RUN) * owned + which
            q, i_q = divmod(i * far_count + j, quarter)
            picks[0, q, i_q : i_q + 1, :] = (lane == at).astype(jnp.float32)

    for (dy, dz, dc), (to_w, to_n, _) in zip(AROUND[1:], members[1:]):
        first, count = taken(dy, dz)
        send(
            picks.at[0, pl.ds(first, count)],
            picks.at[AROUND.index((-dy, -dz, dc)), pl.ds(first, count)],
            2,
            to_w,
            to_n,
        )
    for r in range(rows_here):
        for c in range(cols_here):
            padded[r + 1, c + 1] = field_ref[r, c]

    def run_rows(at):
        return pl.ds(pl.multiple_of(at * planes * tile, planes * tile), planes * tile)

    gathered_here = slices.at[run_rows(x)]
    pltpu.make_async_copy(gathered_here, gathered_here, sem(1)).wait()
    for t in (2, 1, 3):
        pltpu.make_async_remote_copy(
            src_ref=gathered_here,
            dst_ref=gathered_here,
            send_sem=sem(16),
            recv_sem=sem(17),
            device_id=(plane * RUN + beside(t), n),
            device_id_type=MESH,
        ).start()
    other_runs = slices.at[pl.ds(0, (RUN - 1) * planes * tile)]

    copies[4].wait()
    for b in range(blocks):
        r, c = b // cols_here, b % cols_here
        for k in range(near_count):
            number = near_ref[r, c, k]
            grid_cols = cols_here * narrow_count
            row = number // grid_cols - w * rows_here + 1
            row = jnp.where(row < 0, row + rows_here * wide_count, row)
            row = jnp.where(row > rows_here + 1, row - rows_here * wide_count, row)
            col = lax.rem(number, grid_cols) - n * cols_here + 1
            col = jnp.where(col < 0, col + grid_cols, col)
            col = jnp.where(col > cols_here + 1, col - grid_cols, col)
            row, col = jnp.clip(row, 0, rows_here + 1), jnp.clip(col, 0, cols_here + 1)
            spots[b * near_count + k] = row * (cols_here + 2) + col

    for i in (1, 2, 3, 8, 9, 10):
        copies[i].wait()
    for b in range(blocks):
        gain = lax.dot_general(
            whiten_ref[b], whiten_ref[b], TN, precision=EXACT, preferred_element_type=jnp.float32
        )
        gains[b] = gain
        gain_high[b], gain_low[b] = two(gain)
    for j in range(owned):
        white = lax.dot_general(
            coarse_ref[j], coarse_whiten_ref[j], NT, precision=EXACT,
            preferred_element_type=jnp.float32,
        )
        prior = lax.dot_general(
            white, coarse_whiten_ref[j], NN, precision=EXACT, preferred_element_type=jnp.float32
        )
        coarse_out[j] = (
            weibull(coarse_ref[j], coarse_counts_ref[j : j + 1, :], coarse_offset_ref[j : j + 1, :])
            - prior
        )
    for b in range(blocks):
        r, c = b // cols_here, b % cols_here
        fine_out[r, c] = weibull(
            field_ref[r, c], counts_ref[b : b + 1, :], offset_ref[b : b + 1, :]
        )
        weight_copies[b].wait()
        weights_high[b], weights_low[b] = two(weights[b])
        reach = dot_split(gains[b], weights_high[b, :, near_sites:], weights_low[b, :, near_sites:], NN)
        reach_high[b], reach_low[b] = two(reach)
        back_near[b, near_count] = jnp.zeros((chains, sites), jnp.float32)

    arrived(5, 1)
    for e in (0, far_r):
        send(padded.at[e, cols_here], padded.at[e, 0], 22, w, right)
        send(padded.at[e, 1], padded.at[e, far_c], 22, w, left)

    pltpu.make_async_copy(other_runs, other_runs, sem(17)).wait()
    other_picks = picks.at[pl.ds(0, SLICES - 1)]
    pltpu.make_async_copy(other_picks, other_picks, sem(3)).wait()
    held = jnp.concatenate(
        [slices[pl.ds(r, coarse_total, stride=piece), :] for r in range(piece)], axis=1
    )
    for e, (dy, dz, _) in enumerate(AROUND):
        first, count = taken(-dy, -dz)
        for q in range(count):
            row = (STARTS[e] + q) * quarter
            all_picks[row : row + quarter, :] = picks[e, first + q, :quarter, :]
    pick = all_picks[...].astype(jnp.bfloat16)
    chosen = dot_pick(pick, held, NN)
    for r in range(piece):
        far_send[pl.ds(r, SLICES * reads, stride=piece), :] = chosen[:, r * sites : (r + 1) * sites]

    rows_part = quarter * piece

    def by_slice(ref, s, first, count):
        row = pl.multiple_of(s * message + first * rows_part, rows_part)
        return ref.at[pl.ds(row, count * rows_part)]

    def by_device(ref, e, count):
        return ref.at[pl.ds(STARTS[e] * rows_part, count * rows_part)]

    pltpu.make_async_copy(
        by_device(far_send, 0, PARTS), by_slice(far_recv, mine, 0, PARTS), sem(7)
    ).start()
    for e in reversed(range(1, len(AROUND))):
        (dy, dz, _), (to_w, to_n, _) = AROUND[e], members[e]
        first, count = taken(-dy, -dz)
        send(by_device(far_send, e, count), by_slice(far_recv, mine, first, count), 6, to_w, to_n)

    arrived(21, 2)
    arrived(23, 1)
    width = cols_here + 2
    for b in range(blocks):
        r, c = b // cols_here, b % cols_here
        fields = []
        for k in range(near_count):
            spot = spots[b * near_count + k]
            fields.append(padded[spot // width, lax.rem(spot, width)])
        near = jnp.concatenate(fields, axis=1)
        resid[b] = field_ref[r, c] - dot_split(
            near, weights_high[b, :, :near_sites], weights_low[b, :, :near_sites], NT
        )

    pltpu.make_async_copy(far_recv, far_recv, sem(7)).wait()
    for s in range(SLICES):
        for i in range(reads):
            far[i, s * piece : (s + 1) * piece, :] = far_recv[
                s * message + i * piece : s * message + (i + 1) * piece, :
            ]
    for b in range(blocks):
        distant = jnp.concatenate([far[b * far_count + j] for j in range(far_count)], axis=1)
        resid[b] = resid[b] - dot_split(
            distant, weights_high[b, :, near_sites:], weights_low[b, :, near_sites:], NT
        )
    for b in range(blocks):
        back = dot_split(resid[b], reach_high[b], reach_low[b], NN)
        for j in range(far_count):
            i = b * far_count + j
            for s in range(SLICES):
                terms_send[s * message + i * piece : s * message + (i + 1) * piece, :] = back[
                    s * piece : (s + 1) * piece, j * sites : (j + 1) * sites
                ]
    pltpu.make_async_copy(
        by_slice(terms_send, mine, 0, PARTS), by_device(terms_recv, 0, PARTS), sem(9)
    ).start()
    for (dy, dz, dc), (to_w, to_n, s) in zip(AROUND[:0:-1], members[:0:-1]):
        first, count = taken(dy, dz)
        there = AROUND.index((-dy, -dz, dc))
        send(
            by_slice(terms_send, s, first, count), by_device(terms_recv, there, count), 8, to_w, to_n
        )

    for b in range(blocks):
        back_white[b] = dot_split(resid[b], gain_high[b], gain_low[b], NN)
    for b in range(blocks):
        back = dot_split(
            back_white[b], weights_high[b, :, :near_sites], weights_low[b, :, :near_sites], NN
        )
        for k in range(near_count):
            back_near[b, k] = back[:, k * sites : (k + 1) * sites]
    for pr in range(rows_here + 2):
        for pc in range(cols_here + 2):
            total = None
            for b in range(blocks):
                r, c = b // cols_here + 1, b % cols_here + 1
                if max(abs(r - pr), abs(c - pc)) != 1:
                    continue
                slot = jnp.int32(near_count)
                for k in range(near_count):
                    slot = jnp.where(
                        spots[b * near_count + k] == pr * width + pc, jnp.int32(k), slot
                    )
                term = back_near[b, slot]
                total = term if total is None else total + term
            rim[pr, pc] = total
    for e in (0, far_r):
        send(rim.at[e, far_c], rim_in.at[e, 0], 10, w, right)
        send(rim.at[e, 0], rim_in.at[e, far_c], 10, w, left)
    send(rim.at[rows_mid, far_c], rim_in.at[rows_mid, 0], 24, w, right)
    send(rim.at[rows_mid, 0], rim_in.at[rows_mid, far_c], 24, w, left)

    pltpu.make_async_copy(terms_recv, terms_recv, sem(9)).wait()
    gathered = jnp.concatenate(
        [terms_recv[pl.ds(r, SLICES * reads, stride=piece), :] for r in range(piece)], axis=1
    )
    summed = dot_pick(pick, gathered, TN)
    for r in range(piece):
        sums[pl.ds(r, coarse_total, stride=piece), :] = summed[:, r * sites : (r + 1) * sites]

    pltpu.make_async_copy(sums.at[run_rows(x)], sums_beside.at[x], sem(19)).start()
    for t in (2, 1, 3):
        pltpu.make_async_remote_copy(
            src_ref=sums.at[run_rows(beside(t))],
            dst_ref=sums_beside.at[x],
            send_sem=sem(18),
            recv_sem=sem(19),
            device_id=(plane * RUN + beside(t), n),
            device_id_type=MESH,
        ).start()

    arrived(11, 1)
    for e in (0, far_r):
        rim[e, 1] = rim[e, 1] + rim_in[e, 0]
        rim[e, cols_here] = rim[e, cols_here] + rim_in[e, far_c]
    send(rim.at[far_r, cols_mid], rim_in.at[0, cols_mid], 26, up, n)
    send(rim.at[0, cols_mid], rim_in.at[far_r, cols_mid], 26, down, n)

    pltpu.make_async_copy(sums_beside, sums_beside, sem(19)).wait()
    plane_sums[...] = jnp.sum(sums_beside[...], axis=0).reshape(planes, tile, sites)
    pltpu.make_async_copy(plane_sums.at[plane], sums_in.at[plane], sem(13)).start()

    def send_sums(t, carry):
        pltpu.make_async_remote_copy(
            src_ref=plane_sums.at[across(t)],
            dst_ref=sums_in.at[plane],
            send_sem=sem(12),
            recv_sem=sem(13),
            device_id=(across(t) * RUN + x, column(across(t))),
            device_id_type=MESH,
        ).start()
        return carry

    lax.fori_loop(1, planes, send_sums, 0)

    arrived(25, 2)
    arrived(27, 1)
    for r in range(rows_here):
        for c in range(cols_here):
            total = fine_out[r, c] - back_white[r * cols_here + c] + rim[r + 1, c + 1]
            for e, at in ((0, 0), (far_r, rows_here - 1)):
                if r == at:
                    total = total + rim_in[e, c + 1]
            for e, at in ((0, 0), (far_c, cols_here - 1)):
                if c == at:
                    total = total + rim_in[r + 1, e]
            fine_out[r, c] = total

    pltpu.make_async_copy(sums_in, sums_in, sem(13)).wait()
    totals[n] = jnp.sum(
        sums_in[...].reshape(planes // 4, 2, 2, tile, sites), axis=(0, 2)
    )
    for t in range(1, narrow_count):
        pltpu.make_async_remote_copy(
            src_ref=totals.at[n],
            dst_ref=totals.at[n],
            send_sem=sem(14),
            recv_sem=sem(15),
            device_id=(w, lax.rem(n + t, narrow_count)),
            device_id_type=MESH,
        ).start()
    other_totals = totals.at[pl.ds(0, narrow_count - 1)]
    pltpu.make_async_copy(other_totals, other_totals, sem(15)).wait()
    for s in range(SLICES):
        for j in range(owned):
            rows = slice(s * piece, (s + 1) * piece)
            coarse_out[j, rows, :] = (
                coarse_out[j, rows, :]
                + totals[s % 4, s // 4, j * piece : (j + 1) * piece, :]
                + totals[s % 4 + 4, s // 4, j * piece : (j + 1) * piece, :]
            )

    sent = sums_in.at[pl.ds(0, planes - 1)]
    pltpu.make_async_copy(sent, sent, sem(0)).wait()
    pltpu.make_async_copy(other_runs, other_runs, sem(16)).wait()
    pltpu.make_async_copy(other_runs, other_runs, sem(18)).wait()
    pltpu.make_async_copy(other_picks, other_picks, sem(2)).wait()
    others = far_send.at[pl.ds(0, (SLICES - 1) * message)]
    pltpu.make_async_copy(others, others, sem(6)).wait()
    pltpu.make_async_copy(others, others, sem(8)).wait()
    for i, rows in ((4, 1), (20, 2), (22, 1), (10, 1), (24, 2), (26, 1)):
        arrived(i, rows)
    pltpu.make_async_copy(sent, sent, sem(12)).wait()

    pltpu.make_async_copy(other_totals, other_totals, sem(14)).wait()


def per_device(
    wide_count,
    narrow_count,
    fine_field,
    fine_counts,
    fine_offset,
    kriging,
    whiten,
    neighbours,
    coarse_list,
    coarse_field,
    coarse_counts,
    coarse_offset,
    coarse_whiten,
    coarse_home,
):
    rows_here, cols_here, chains, sites = fine_field.shape
    blocks = rows_here * cols_here
    owned = coarse_field.shape[0]
    cond = kriging.shape[3]
    near_count, far_count = neighbours.shape[2], coarse_list.shape[2]
    reads = blocks * far_count
    piece = chains // SLICES
    f32, bf16 = jnp.float32, jnp.bfloat16
    vmem = pl.BlockSpec(memory_space=pltpu.VMEM)
    operands = (
        fine_field,
        fine_counts.reshape(blocks, sites),
        fine_offset.reshape(blocks, sites),
        whiten.reshape(blocks, sites, sites),
        neighbours,
        coarse_list.transpose(2, 1, 0),
        coarse_home,
        coarse_field,
        coarse_counts,
        coarse_offset,
        coarse_whiten,
    )
    return pl.pallas_call(
        functools.partial(kernel, wide_count, narrow_count),
        out_shape=(
            pltpu.VMEM(fine_field.shape, f32),
            pltpu.VMEM(coarse_field.shape, f32),
        ),
        in_specs=[pl.BlockSpec(memory_space=pltpu.HBM)] * (1 + len(operands)),
        out_specs=(vmem, vmem),
        scratch_shapes=[
            (pltpu.SMEM if i in (4, 5, 6) else pltpu.VMEM)(x.shape, x.dtype)
            for i, x in enumerate(operands)
        ]
        + [
            pltpu.VMEM((blocks, sites, cond), f32),
            pltpu.VMEM((blocks, sites, cond), bf16),
            pltpu.VMEM((blocks, sites, cond), bf16),
            pltpu.VMEM((blocks, sites, sites), bf16),
            pltpu.VMEM((blocks, sites, sites), bf16),
            pltpu.VMEM((blocks, sites, sites), f32),
            pltpu.VMEM((blocks, sites, far_count * sites), bf16),
            pltpu.VMEM((blocks, sites, far_count * sites), bf16),
            pltpu.VMEM((rows_here + 2, cols_here + 2, chains, sites), f32),
            pltpu.VMEM((rows_here + 2, cols_here + 2, chains, sites), f32),
            pltpu.VMEM((rows_here + 2, cols_here + 2, chains, sites), f32),
            pltpu.VMEM((SLICES, owned * piece, sites), f32),
            pltpu.VMEM((wide_count * owned * piece, sites), f32),
            pltpu.VMEM((len(AROUND), PARTS, 8, wide_count * owned), f32),
            pltpu.VMEM((reads * SLICES, wide_count * owned), f32),
            pltpu.VMEM((SLICES * reads * piece, sites), f32),
            pltpu.VMEM((SLICES * reads * piece, sites), f32),
            pltpu.VMEM((reads, chains, sites), f32),
            pltpu.VMEM((blocks, near_count + 1, chains, sites), f32),
            pltpu.VMEM((blocks, chains, sites), f32),
            pltpu.VMEM((blocks, chains, sites), f32),
            pltpu.VMEM((SLICES * reads * piece, sites), f32),
            pltpu.VMEM((SLICES * reads * piece, sites), f32),
            pltpu.VMEM((wide_count * owned * piece, sites), f32),
            pltpu.VMEM((RUN, wide_count // RUN * owned * piece, sites), f32),
            pltpu.VMEM((wide_count // RUN, owned * piece, sites), f32),
            pltpu.VMEM((wide_count // RUN, owned * piece, sites), f32),
            pltpu.VMEM((narrow_count, 2, owned * piece, sites), f32),
            pltpu.SMEM((blocks * near_count,), jnp.int32),
            pltpu.SemaphoreType.DMA((blocks,)),
            pltpu.SemaphoreType.DMA((28,)),
            pltpu.SemaphoreType.DMA((len(operands),)),
        ],
        compiler_params=pltpu.CompilerParams(
            collective_id=0, has_side_effects=True, vmem_limit_bytes=60 * 1024 * 1024
        ),
    )(kriging.reshape(blocks, sites, cond), *operands)


def solution(mesh):
    return jax.shard_map(
        functools.partial(per_device, mesh.shape["wide"], mesh.shape["narrow"]),
        mesh=mesh,
        in_specs=(
            P("wide", "narrow", None, None),
            P("wide", "narrow", None),
            P("wide", "narrow", None),
            P("wide", "narrow", None, None),
            P("wide", "narrow", None, None),
            P("wide", "narrow", None),
            P("wide", "narrow", None),
            P("wide", None, None),
            P("wide", None),
            P("wide", None),
            P("wide", None, None),
            P(),
        ),
        out_specs=(P("wide", "narrow", None, None), P("wide", None, None)),
        check_vma=False,
    )
```
